256 devices in a mesh: vis: 64 (over x, z, core), tile: 4 (over y).
Axes of the slice: x: 4, y: 4, z: 8, core: 2. Of those that a mesh axis runs over, the one named last changes fastest.
Arguments:
- vis_data: bfloat16 [262144, 128], P(('vis', 'tile')), may hold values from -0.59765625 to 0.59765625
- u_cell: int32 [16, 262144], P(None, ('vis', 'tile')), may hold values from 0 to 25
- v_cell: int32 [16, 262144], P(None, ('vis', 'tile')), may hold values from 0 to 25
- u_frac: int32 [16, 262144], P(None, ('vis', 'tile')), may hold values from 0 to 15
- v_frac: int32 [16, 262144], P(None, ('vis', 'tile')), may hold values from 0 to 15
- w_plane: int32 [16, 262144], P(None, ('vis', 'tile')), may hold values from 0 to 7
- block_route: int32 [262144, 1], P(('vis', 'tile')), may hold values from 0 to 511; in each aligned block of 1024 rows (0 to 1023, 1024 to 2047, ...) at most 4 rows name the same one
- kernel_taps: float32 [128, 7], replicated, may hold values from 0.1 to 1
- taper_gain: float32 [32, 32], replicated, may hold values from 0.2 to 1
- sub_tile: int32 [2048, 1], P(('vis', 'tile')), may hold values from 0 to 7; in each aligned block of 8 rows (0 to 7, 8 to 15, ...) at most 2 rows name the same one
- sub_anchor: int32 [2048, 2], P(('vis', 'tile')), may hold values from 0 to 224
Outputs:
- grid_sum: float32 [8, 256, 2048], P('tile', 'vis')
The draws below stay inside these ranges and needn't reach their ends.
Inputs may be any that keep to these rules, and one draw needn't show every extreme that they name: `block_route`: among the rows of one device at most 4 name one uv-block, and some uv-block is named by exactly 4 of them. `sub_tile`: among the 8 uv-blocks of one device at most 2 map to one grid tile, and some grid tile gets exactly 2 of them.
All inputs are finite; a program needn't handle non-finite values.
Results may differ from the reference program's by a relative error of at most 0.008.
Values may be sent and summed in bfloat16 or wider, within the bound.
No kernel may reach another device: no remote copies, remote signals or barrier semaphores. Data moves between devices by JAX's collectives and lax.ppermute only.
A program may use at most 128 MiB of HBM per device.

```python
import math
import jax
import jax.numpy as jnp
import numpy as np
from jax import lax

ROWS_DEV = 1024
BLK_DEV = 8
SUB = 32
CHR = 16
POLC = 8
TAPS = 7
OS = 16
WPL = 8
TS = 256
SCAP = 2
NGROUP = 512
CAP = 4
GT = 8
NROWS = 262144
NBLK = 2048
N_VIS = 64
N_TILE = 4
DEVICES = 256


def place_ends(array, key, least, top_value):
    spot = [jax.random.randint(jax.random.fold_in(key, axis), (), 0, length) for axis, length in enumerate(array.shape)]
    widest = array.shape.index(max(array.shape))
    beside = spot[:widest] + [(spot[widest] + 1) % array.shape[widest]] + spot[widest + 1:]
    return array.at[tuple(spot)].set(least).at[tuple(beside)].set(top_value)


def steps_of(own_key, dims, pieces, least, high):
    level, own = 1.0, jax.random.fold_in(own_key, 6)
    for axis_at, parts in pieces:
        steps = jnp.exp(jax.random.uniform(jax.random.fold_in(own, axis_at), (parts,), jnp.float32, least / len(pieces), high / len(pieces)))
        level = level * jnp.repeat(steps, dims[axis_at] // parts).reshape([-1 if axis == axis_at else 1 for axis in range(len(dims))])
    return level


def routed_block(rng, own, number, rows, amount, top, bound, slope):
    ranking = jax.random.permutation(rng, amount)
    heavy_load, ordinary = load_shares(amount, rows * top, bound, slope, True), load_shares(amount, rows * top, bound, slope, False)
    places = jnp.arange(amount)

    def named(tallies, rotation):
        used = int((tallies > 0).sum())
        fixed = max(1, used // 4)
        shifted = fixed + (places - fixed + rotation * (used - fixed)) % max(1, amount - fixed)
        return jnp.zeros((amount,), jnp.int32).at[ranking[jnp.where(places < fixed, places, shifted)]].set(jnp.asarray(tallies, jnp.int32))

    tallies = jnp.where(number % 4 == 0, named(heavy_load, number // 4), named(ordinary, number - number // 4 - 1))
    mixed = jax.random.permutation(jax.random.fold_in(own, 3), amount)
    donor, sink = mixed[0:amount // 2 * 2:2], mixed[1:amount // 2 * 2:2]
    slack = jnp.minimum(tallies[donor] - 1, bound - tallies[sink]) // 2
    slack = jnp.where((donor == ranking[0]) | (sink == ranking[0]) | (tallies[sink] == 0), 0, jnp.maximum(slack, 0))
    shifted = jax.random.randint(jax.random.fold_in(own, 4), (amount // 2,), 0, 1 << 20) % (slack + 1)
    tallies = tallies.at[donor].add(-shifted).at[sink].add(shifted)
    items = jnp.searchsorted(jnp.cumsum(tallies), jnp.arange(rows * top), side="right").astype(jnp.int32)
    grid = items.reshape(top, rows).T
    grid = grid[jax.random.permutation(jax.random.fold_in(own, 1), rows)]
    rotation = jax.random.randint(jax.random.fold_in(own, 2), (rows, 1), 0, top)
    return jnp.take_along_axis(grid, (jnp.arange(top)[None, :] + rotation) % top, axis=1)


def load_shares(number_of, total, bound, skew, full):
    portions = [(1 << 20) // math.isqrt(standing ** skew) + 1 for standing in range(1, number_of + 1)]
    largest = bound if full else min(bound, max(-(-total // number_of), total * portions[0] // sum(portions)))
    least = 1 if total - largest >= number_of - 1 else 0
    holding, surplus = [largest] + [least] * (number_of - 1), total - largest - least * (number_of - 1)
    while surplus > 0:
        candidates = [i for i in range(1, number_of) if holding[i] < largest] or [i for i in range(1, number_of) if holding[i] < bound]
        mass, budget = sum([portions[i] for i in candidates]), surplus
        for i in candidates:
            addition = min(bound - holding[i], max(1, budget * portions[i] // mass), surplus)
            holding[i] = holding[i] + addition
            surplus = surplus - addition
    return np.array(holding)


def centred(key, shape, scale, bound, shards=(), kind=jnp.bfloat16):
    result = scale * jax.random.normal(key, shape, jnp.float32)
    if shards:
        result = result * steps_of(key, shape, shards, -0.22, 0.18)
    return jnp.clip(result, -bound, bound).astype(kind)


def setup_inputs(seed: int = 0) -> dict:
    keys = jax.random.split(jax.random.key(seed), 12)
    vis_data = centred(keys[0], (NROWS, CHR * POLC), 0.1, 0.59765625, ((0, 256),))
    u_cell = place_ends(jax.random.randint(keys[1], (CHR, NROWS), 0, SUB - TAPS + 1), jax.random.fold_in(keys[1], 1), 0, SUB - TAPS).astype(jnp.int32)
    v_cell = place_ends(jax.random.randint(keys[2], (CHR, NROWS), 0, SUB - TAPS + 1), jax.random.fold_in(keys[2], 1), 0, SUB - TAPS).astype(jnp.int32)
    u_frac = place_ends(jax.random.randint(keys[3], (CHR, NROWS), 0, OS), jax.random.fold_in(keys[3], 1), 0, OS - 1).astype(jnp.int32)
    v_frac = place_ends(jax.random.randint(keys[4], (CHR, NROWS), 0, OS), jax.random.fold_in(keys[4], 1), 0, OS - 1).astype(jnp.int32)
    w_plane = place_ends(jax.random.randint(keys[5], (CHR, NROWS), 0, WPL), jax.random.fold_in(keys[5], 1), 0, WPL - 1).astype(jnp.int32)
    block_route_keys = jax.random.split(jax.random.fold_in(keys[6], 1), NROWS // ROWS_DEV)
    block_route_turns = jax.random.permutation(jax.random.fold_in(keys[6], 3), NROWS // ROWS_DEV)
    block_route = jax.vmap(lambda own, number: routed_block(jax.random.fold_in(keys[6], 2), own, number, ROWS_DEV, NGROUP, 1, CAP, 2))(block_route_keys, block_route_turns).reshape((NROWS, 1))
    kernel_taps = jnp.clip(jax.random.uniform(keys[7], (WPL * OS, TAPS), jnp.float32, 0.1, 1.0), 0.1, 1.0)
    taper_gain = jnp.clip(jax.random.uniform(keys[8], (SUB, SUB), jnp.float32, 0.2, 1.0), 0.2, 1.0)
    sub_tile_keys = jax.random.split(jax.random.fold_in(keys[9], 1), NBLK // BLK_DEV)
    sub_tile_turns = jax.random.permutation(jax.random.fold_in(keys[9], 3), NBLK // BLK_DEV)
    sub_tile = jax.vmap(lambda own, number: routed_block(jax.random.fold_in(keys[9], 2), own, number, BLK_DEV, GT, 1, SCAP, 2))(sub_tile_keys, sub_tile_turns).reshape((NBLK, 1))
    sub_anchor = place_ends(jax.random.randint(keys[10], (NBLK, 2), 0, TS - SUB + 1), jax.random.fold_in(keys[10], 1), 0, TS - SUB).astype(jnp.int32)
    return {"vis_data": vis_data, "u_cell": u_cell, "v_cell": v_cell, "u_frac": u_frac, "v_frac": v_frac, "w_plane": w_plane, "block_route": block_route, "kernel_taps": kernel_taps, "taper_gain": taper_gain, "sub_tile": sub_tile, "sub_anchor": sub_anchor}


def spread(cell_idx, taps):
    offset = jnp.arange(SUB, dtype=jnp.int32)[None, :] - cell_idx[:, None]
    spread_sum = jnp.zeros((cell_idx.shape[0], SUB), jnp.float32)
    for tap_index in range(TAPS):
        spread_sum = spread_sum + jnp.where(offset == tap_index, taps[:, tap_index:tap_index + 1], 0.0)
    return spread_sum.astype(jnp.bfloat16)


def grid_block(samples, code_rows, kernel_taps, taper_gain):
    taps_u = kernel_taps[code_rows[2]]
    taps_v = kernel_taps[code_rows[3]]
    weight_u = spread(code_rows[0], taps_u)
    weight_v = spread(code_rows[1], taps_v)
    weighted = (weight_u.astype(jnp.float32)[:, :, None] * samples.astype(jnp.float32)[:, None, :]).astype(jnp.bfloat16)
    weighted = weighted.reshape(samples.shape[0], SUB * POLC)
    subgrid = jnp.dot(weight_v.T, weighted, preferred_element_type=jnp.float32)
    return subgrid * jnp.repeat(taper_gain, POLC, axis=1)


def place_tiles(canvas, sub_grids, tile_ids, anchors, first_tile):
    tile_count = canvas.shape[0]

    def add_one(slot_index, canvas):
        target = (tile_ids[slot_index] - first_tile).astype(jnp.int32)
        inside = (target >= 0) & (target < tile_count)
        target = jnp.clip(target, 0, tile_count - 1).astype(jnp.int32)
        corner = (target, anchors[slot_index, 0].astype(jnp.int32), (anchors[slot_index, 1] * POLC).astype(jnp.int32))
        window = lax.dynamic_slice(canvas, corner, (1, SUB, SUB * POLC))
        addend = jnp.where(inside, sub_grids[slot_index], 0.0)[None]
        return lax.dynamic_update_slice(canvas, window + addend, corner)

    return lax.fori_loop(0, sub_grids.shape[0], add_one, canvas)


def rank_rows(row_route):
    onehot = (row_route[:, None] == jnp.arange(NGROUP, dtype=jnp.int32)[None, :]).astype(jnp.int32)
    before = jnp.cumsum(onehot, axis=0) - onehot
    return jnp.sum(before * onehot, axis=1).astype(jnp.int32)


def reference(vis_data, u_cell, v_cell, u_frac, v_frac, w_plane, block_route, kernel_taps, taper_gain, sub_tile, sub_anchor):
    flat_route = block_route[:, 0].astype(jnp.int32)
    row_rank = lax.map(rank_rows, flat_route.reshape(DEVICES, ROWS_DEV)).reshape(-1)
    device = jnp.arange(NROWS, dtype=jnp.int32) // ROWS_DEV
    vis_index = device // N_TILE
    tile_index = device % N_TILE
    block_id = ((flat_route // BLK_DEV) * N_TILE + tile_index) * BLK_DEV + flat_route % BLK_DEV
    slot_id = vis_index * CAP + row_rank
    slot_table = jnp.full((NBLK, N_VIS * CAP), -1, jnp.int32).at[block_id, slot_id].set(jnp.arange(NROWS, dtype=jnp.int32))
    table_u = w_plane * OS + u_frac
    table_v = w_plane * OS + v_frac
    codes_all = jnp.stack([u_cell.T, v_cell.T, table_u.T, table_v.T], axis=1).astype(jnp.int32)

    def grid_one(slot_rows):
        is_live = slot_rows >= 0
        safe_rows = jnp.maximum(slot_rows, 0)
        samples = jnp.where(is_live[:, None], vis_data[safe_rows], jnp.zeros((), jnp.bfloat16))
        samples = samples.reshape(-1, POLC)
        code_rows = jnp.transpose(codes_all[safe_rows], (1, 0, 2)).reshape(4, -1)
        return grid_block(samples, code_rows, kernel_taps, taper_gain)

    subgrids = lax.map(grid_one, slot_table)
    canvas = jnp.zeros((GT, TS, TS * POLC), jnp.float32)
    return place_tiles(canvas, subgrids, sub_tile[:, 0].astype(jnp.int32), sub_anchor, 0)
```

```python
import jax
import jax.numpy as jnp
from jax import lax
from jax.experimental import pallas as pl
from jax.experimental.pallas import tpu as pltpu
from jax.sharding import Mesh
from jax.sharding import PartitionSpec as P

ROWS = 1024
BLK = 8
SUB = 32
CHR = 16
POLC = 8
TAPS = 7
OS = 16
CAP = 4
N_VIS = 64
SLOTS = BLK * CAP
COLS = 256
DATA = CHR * POLC
PIECES = 128
FLAT = 4 * 256
WIDE = FLAT + 128
VIS = ("x", "zh", "zl", "core")
BF = jnp.bfloat16
F32 = jnp.float32
I32 = jnp.int32
VMEM_BYTES = 48 * 1024 * 1024


def pack_kernel(route_ref, vis_ref, uc_ref, vc_ref, uf_ref, vf_ref, w_ref, out_ref):
    route = route_ref[...]
    column = jnp.transpose(jnp.broadcast_to(route.astype(F32), (8, ROWS)))[:, 0:1]
    route_f = route.astype(F32)
    rank = jnp.zeros((1, ROWS), F32)
    step = 128
    for start in range(0, ROWS, step):
        mine = column[start : start + step]
        earlier = lax.broadcasted_iota(I32, (step, ROWS), 0) + start < lax.broadcasted_iota(
            I32, (step, ROWS), 1
        )
        same = jnp.where((mine == route_f) & earlier, 1.0, 0.0)
        rank = rank + jnp.sum(same, axis=0, keepdims=True)
    slot = route * CAP + rank.astype(I32)

    codes = jnp.concatenate(
        [ref[...].astype(F32) for ref in (uc_ref, vc_ref, uf_ref, vf_ref, w_ref)]
        + [jnp.zeros((DATA - 5 * CHR, ROWS), F32)],
        axis=0,
    )
    codes = jnp.transpose(codes).astype(BF)
    data = jnp.concatenate([vis_ref[...], codes], axis=1)

    chunk = 256

    def body(index, carry):
        base = index * chunk
        place = lax.broadcasted_iota(I32, (chunk, ROWS), 0) + base
        onehot = jnp.where(place == slot, 1.0, 0.0).astype(BF)
        packed = jnp.dot(onehot, data, preferred_element_type=F32)
        out_ref[pl.ds(pl.multiple_of(base, chunk), chunk), :] = packed.astype(BF)
        return carry

    lax.fori_loop(0, N_VIS * SLOTS // chunk, body, 0)


def grid_kernel(
    tile_ref, anchor_ref, recv_ref, taps_ref, taper_ref, out_ref, wide, turned, wd, wv, rolled, send
):
    for side in range(2):
        wide[side] = recv_ref[:, side * 128 : side * 128 + 128].astype(F32)
    send[...] = jnp.zeros_like(send)
    taps = taps_ref[...]
    lane = lax.broadcasted_iota(I32, (8, 128), 1)
    sub8 = lax.broadcasted_iota(I32, (8, 128), 0)

    def one_block(block, carry):
        for side in range(2):
            parts = [
                wide[side, pl.ds(block * CAP + r, N_VIS, stride=SLOTS), :] for r in range(CAP)
            ]
            turned[side * 128 : side * 128 + 128, :] = jnp.transpose(
                jnp.concatenate(parts, axis=0)
            )

        for h in range(CHR):
            for half in range(2):
                at = slice(half * 128, half * 128 + 128)
                to = slice(h * 256 + half * 128, h * 256 + half * 128 + 128)

                def code(kind):
                    row = DATA + kind * CHR + h
                    return jnp.broadcast_to(turned[row : row + 1, at], (8, 128)).astype(I32)

                u_cell, v_cell, u_frac, v_frac, plane = [code(k) for k in range(5)]
                taps_u = jnp.take_along_axis(taps, plane * OS + u_frac, axis=1)
                taps_v = jnp.take_along_axis(taps, plane * OS + v_frac, axis=1)
                samples = turned[h * POLC : (h + 1) * POLC, at]
                rows_v = []
                for group in range(SUB // 8):
                    tap = sub8 + group * 8 - v_cell
                    tap = jnp.where((tap >= 0) & (tap < TAPS), tap, TAPS)
                    rows_v.append(jnp.take_along_axis(taps_v, tap, axis=0))
                wv[:, to] = jnp.concatenate(rows_v, axis=0).astype(BF)
                rows_u = []
                for u in range(SUB):
                    tap = u - u_cell
                    tap = jnp.where((tap >= 0) & (tap < TAPS), tap, TAPS)
                    rows_u.append(jnp.take_along_axis(taps_u, tap, axis=0) * samples)
                wd[:, to] = jnp.concatenate(rows_u, axis=0).astype(BF)

        total = lax.dot_general(
            wv[...], wd[...], (((1,), (1,)), ((), ())), preferred_element_type=F32
        )
        total = total * taper_ref[...]
        anchor_v, anchor_u = anchor_ref[block, 0], anchor_ref[block, 1]
        shift_v = lax.rem(anchor_v, SUB)
        shift_u = lax.rem(anchor_u, SUB) * POLC
        total = pltpu.roll(total, shift_v, 0)
        total = pltpu.roll(total, shift_u, 1)
        for side in range(2):
            rolled[side] = total[:, side * 128 : side * 128 + 128]
        tile = tile_ref[block, 0]
        group = lax.div(tile, 2)
        order = lax.fori_loop(
            0,
            block,
            lambda other, n: n + jnp.where(lax.div(tile_ref[other, 0], 2) == group, 1, 0),
            0,
        )
        row = group * CAP + order
        for k in range(4):
            for side in range(2):
                send[k * 2 + side, pl.ds(row, 8, stride=16), :] = rolled[
                    side, pl.ds(k, 8, stride=4), :
                ]
        meta = jnp.where(lane == 0, 1 + lax.rem(tile, 2), 0)
        meta = jnp.where(lane == 1, lax.div(anchor_v, SUB), meta)
        meta = jnp.where(lane == 2, shift_v - 4 * sub8, meta)
        meta = jnp.where(lane == 3, lax.div(anchor_u, SUB), meta)
        meta = jnp.where(lane == 4, shift_u, meta)
        send[8, pl.ds(row, 8, stride=16), :] = meta.astype(F32)
        return carry

    lax.fori_loop(0, BLK, one_block, 0)
    for part in range(WIDE // 128):
        out_ref[:, part * 128 : part * 128 + 128] = send[part].astype(BF)


def place_kernel(recv_ref, out_ref):
    meta = recv_ref[:, FLAT:WIDE].astype(F32)
    kind, row_y, edge_v, row_x, edge_u = [
        meta[:, k : k + 1].astype(I32) for k in range(5)
    ]
    data = recv_ref[:, :FLAT].astype(F32)
    spot = lax.broadcasted_iota(I32, (PIECES, FLAT), 1)
    late_v = lax.shift_right_logical(spot, 8) < edge_v
    late_u = lax.bitwise_and(spot, 255) < edge_u
    target = lax.broadcasted_iota(I32, (PIECES, PIECES), 1)
    first = jnp.where(kind > 0, row_y * 16 + (kind - 1) * 8 + row_x, -64)
    picks, pieces = [], []
    for down in range(2):
        for right in range(2):
            keep_v = late_v if down else jnp.logical_not(late_v)
            keep_u = late_u if right else jnp.logical_not(late_u)
            pieces.append(jnp.where(keep_v & keep_u, data, 0.0).astype(BF))
            picks.append(
                jnp.where(target == first + (16 * down + right), 1.0, 0.0)
            )
    pick = jnp.concatenate(picks, axis=0)
    piece = jnp.concatenate(pieces, axis=0)
    pick = jnp.transpose(pick).astype(BF)
    out_ref[...] = jnp.dot(pick, piece, preferred_element_type=F32).astype(BF)


def total_kernel(recv_ref, out_ref):
    total = recv_ref[0:16, :].astype(F32)
    for source in range(1, 8):
        total = total + recv_ref[source * 16 : source * 16 + 16, :].astype(F32)
    for tile in range(2):
        for across in range(8):
            for k in range(4):
                row = tile * 8 + across
                out_ref[tile, k : k + 1, across * 256 : across * 256 + 256] = total[
                    row : row + 1, k * 256 : k * 256 + 256
                ]


def call(kernel, shape, dtype, spaces, scratch=(), flops=0, moved=0):
    specs = [pl.BlockSpec(memory_space=space) for space in spaces]
    return pl.pallas_call(
        kernel,
        out_shape=jax.ShapeDtypeStruct(shape, dtype),
        in_specs=specs,
        out_specs=pl.BlockSpec(memory_space=pltpu.VMEM),
        scratch_shapes=list(scratch),
        compiler_params=pltpu.CompilerParams(vmem_limit_bytes=VMEM_BYTES),
        cost_estimate=pl.CostEstimate(flops=flops, bytes_accessed=moved, transcendentals=0),
    )


def on_device(
    vis_data,
    u_cell,
    v_cell,
    u_frac,
    v_frac,
    w_plane,
    block_route,
    kernel_taps,
    taper_gain,
    sub_tile,
    sub_anchor,
):
    vm, sm = pltpu.VMEM, pltpu.SMEM
    total_slots = N_VIS * SLOTS
    packed = call(
        pack_kernel, (total_slots, COLS), BF, [vm] * 7, flops=1 << 30, moved=2 << 20
    )(block_route.reshape(1, ROWS), vis_data, u_cell, v_cell, u_frac, v_frac, w_plane)
    rows = lax.all_to_all(
        packed.reshape(N_VIS, SLOTS, COLS), VIS, split_axis=0, concat_axis=0, tiled=True
    ).reshape(total_slots, COLS)

    taps = jnp.zeros((8, 128), F32).at[:TAPS].set(kernel_taps.T.astype(BF).astype(F32))
    taper = jnp.repeat(taper_gain, POLC, axis=1)
    depth = CHR * N_VIS * CAP
    pieces = call(
        grid_kernel,
        (PIECES, WIDE),
        BF,
        [sm, sm, vm, vm, vm],
        scratch=[
            pltpu.VMEM((2, total_slots, 128), F32),
            pltpu.VMEM((COLS, COLS), F32),
            pltpu.VMEM((SUB * POLC, depth), BF),
            pltpu.VMEM((SUB, depth), BF),
            pltpu.VMEM((2, SUB, 128), F32),
            pltpu.VMEM((WIDE // 128, PIECES, 128), F32),
        ],
        flops=1 << 32,
        moved=2 << 20,
    )(sub_tile, sub_anchor, rows, taps, taper)
    pieces = lax.all_to_all(
        pieces.reshape(32, CAP, WIDE),
        ("zl", "core", "tile"),
        split_axis=0,
        concat_axis=0,
        tiled=True,
    ).reshape(PIECES, WIDE)
    canvas = call(place_kernel, (PIECES, FLAT), BF, [vm], flops=1 << 27, moved=1 << 19)(pieces)
    canvas = lax.all_to_all(
        canvas.reshape(8, 16, FLAT), ("x", "zh"), split_axis=0, concat_axis=0, tiled=True
    ).reshape(PIECES, FLAT)
    return call(total_kernel, (2, 4, 2048), F32, [vm], moved=1 << 19)(canvas)


def solution(mesh):
    split = Mesh(
        mesh.devices.reshape(4, 2, 4, 2, 4), ("x", "zh", "zl", "core", "tile")
    )
    every = VIS + ("tile",)
    placed = (
        (P(every, None),)
        + (P(None, every),) * 5
        + (P(every, None), P(), P(), P(every, None), P(every, None))
    )
    return jax.shard_map(
        on_device, mesh=split, in_specs=placed, out_specs=P("tile", VIS, None), check_vma=False
    )
```

```python
import jax
import jax.numpy as jnp
from jax import lax
from jax.experimental import pallas as pl
from jax.experimental.pallas import tpu as pltpu
from jax.sharding import Mesh
from jax.sharding import PartitionSpec as P

ROWS = 1024
BLK = 8
SUB = 32
CHR = 16
POLC = 8
TAPS = 7
OS = 16
CAP = 4
N_VIS = 64
SLOTS = BLK * CAP
COLS = 256
DATA = CHR * POLC
PIECES = 128
FLAT = 4 * 256
WIDE = FLAT + 128
VIS = ("x", "zh", "zl", "core")
BF = jnp.bfloat16
F32 = jnp.float32
I32 = jnp.int32
VMEM_BYTES = 48 * 1024 * 1024


def pack_kernel(route_ref, vis_ref, uc_ref, vc_ref, uf_ref, vf_ref, w_ref, out_ref):
    route = route_ref[...]
    column = jnp.transpose(jnp.broadcast_to(route.astype(F32), (8, ROWS)))[:, 0:1]
    route_f = route.astype(F32)
    rank = jnp.zeros((1, ROWS), F32)
    step = 128
    for start in range(0, ROWS, step):
        mine = column[start : start + step]
        earlier = lax.broadcasted_iota(I32, (step, ROWS), 0) + start < lax.broadcasted_iota(
            I32, (step, ROWS), 1
        )
        same = jnp.where((mine == route_f) & earlier, 1.0, 0.0)
        rank = rank + jnp.sum(same, axis=0, keepdims=True)
    slot = route * CAP + rank.astype(I32)

    codes = jnp.concatenate(
        [ref[...].astype(F32) for ref in (uc_ref, vc_ref, uf_ref, vf_ref, w_ref)]
        + [jnp.zeros((DATA - 5 * CHR, ROWS), F32)],
        axis=0,
    )
    codes = jnp.transpose(codes).astype(BF)
    data = jnp.concatenate([vis_ref[...], codes], axis=1)

    chunk = 256

    def body(index, carry):
        base = index * chunk
        place = lax.broadcasted_iota(I32, (chunk, ROWS), 0) + base
        onehot = jnp.where(place == slot, 1.0, 0.0).astype(BF)
        packed = jnp.dot(onehot, data, preferred_element_type=F32)
        out_ref[pl.ds(pl.multiple_of(base, chunk), chunk), :] = packed.astype(BF)
        return carry

    lax.fori_loop(0, N_VIS * SLOTS // chunk, body, 0)


def grid_kernel(
    tile_ref, anchor_ref, recv_ref, taps_ref, taper_ref, out_ref, wide, turned, codes, rolled, send
):
    for side in range(2):
        wide[side] = recv_ref[:, side * 128 : side * 128 + 128].astype(F32)
    send[...] = jnp.zeros_like(send)
    taps = taps_ref[...]
    lane = lax.broadcasted_iota(I32, (8, 128), 1)
    sub8 = lax.broadcasted_iota(I32, (8, 128), 0)
    rows16 = lax.broadcasted_iota(I32, (16, 128), 0)
    low_lanes = lax.broadcasted_iota(I32, (SUB, 128), 1) < 64
    pair_of = [
        (2 * pair + jnp.where(rows16 < 8, 0, 1)).astype(F32).astype(BF) for pair in range(4)
    ]
    zero16 = jnp.zeros((16, 128), BF)

    def weights(cell_low, index):
        picked = jnp.take_along_axis(taps, jnp.broadcast_to(index, (8, 128)), axis=1)
        return jnp.take_along_axis(picked, (sub8 - cell_low) & 7, axis=0)

    def one_block(block, carry):
        for side in range(2):
            parts = [
                wide[side, pl.ds(block * CAP + r, N_VIS, stride=SLOTS), :] for r in range(CAP)
            ]
            turned[side * 128 : side * 128 + 128, :] = jnp.transpose(
                jnp.concatenate(parts, axis=0)
            )
        u_cell, v_cell, u_frac, v_frac, plane = [
            turned[DATA + kind * CHR : DATA + (kind + 1) * CHR, :].astype(I32)
            for kind in range(5)
        ]
        codes[0] = u_cell & 7
        codes[1] = lax.shift_right_logical(u_cell, 3)
        codes[2] = v_cell & 7
        codes[3] = lax.shift_right_logical(v_cell, 3)
        codes[4] = plane * OS + u_frac
        codes[5] = plane * OS + v_frac

        total = jnp.zeros((128, 128), F32)
        for h in range(CHR):
            a_halves, b_halves = [], []
            for half in range(2):
                at = slice(half * 128, half * 128 + 128)
                u_low, u_high, v_low, v_high, u_index, v_index = [
                    jnp.broadcast_to(codes[kind, h : h + 1, at], (8, 128)) for kind in range(6)
                ]
                turn_u = weights(u_low, u_index)
                turn_v = weights(v_low, v_index)
                samples = turned[h * POLC : (h + 1) * POLC, at]
                group_v = v_high + jnp.where(sub8 < v_low, 1, 0)
                weight_v = [jnp.where(group_v == g, turn_v, 0.0) for g in range(4)]
                weight_v = [
                    jnp.concatenate(weight_v[2 * g : 2 * g + 2], axis=0).astype(BF)
                    for g in range(2)
                ]
                high = u_high.astype(F32)
                high = jnp.concatenate([high, high], axis=0).astype(BF)
                b_rows = []
                for g in range(4):
                    mask = high == jnp.asarray(g, BF)
                    b_rows += [jnp.where(mask, part, zero16) for part in weight_v]
                b_halves.append(jnp.concatenate(b_rows, axis=0))
                low = u_low.astype(F32)
                low = jnp.concatenate([low, low], axis=0).astype(BF)
                same, later = [], []
                for pair in range(4):
                    product = [
                        jnp.broadcast_to(turn_u[s : s + 1], (8, 128)) * samples
                        for s in (2 * pair, 2 * pair + 1)
                    ]
                    product = jnp.concatenate(product, axis=0).astype(BF)
                    mask = low <= pair_of[pair]
                    same.append(jnp.where(mask, product, zero16))
                    later.append(jnp.where(mask, zero16, product))
                a_halves.append(jnp.concatenate(same + later, axis=0))
            total = total + lax.dot_general(
                jnp.concatenate(b_halves, axis=1),
                jnp.concatenate(a_halves, axis=1),
                (((1,), (1,)), ((), ())),
                preferred_element_type=F32,
            )

        crossed = pltpu.roll(total, 64, 1)
        anchor_v, anchor_u = anchor_ref[block, 0], anchor_ref[block, 1]
        shift_v = lax.rem(anchor_v, SUB)
        shift_u = lax.rem(anchor_u, SUB) * POLC
        sides = []
        for side in range(2):
            before = crossed[32:64] if side else jnp.zeros((SUB, 128), F32)
            after = crossed[96:128] if side else crossed[32:64]
            sides.append(total[side * 64 : side * 64 + 32] + jnp.where(low_lanes, before, after))
        grid = jnp.concatenate(sides, axis=1) * taper_ref[...]
        grid = pltpu.roll(grid, shift_v, 0)
        grid = pltpu.roll(grid, shift_u, 1)
        for side in range(2):
            rolled[side] = grid[:, side * 128 : side * 128 + 128]
        tile = tile_ref[block, 0]
        group = lax.div(tile, 2)
        order = lax.fori_loop(
            0,
            block,
            lambda other, n: n + jnp.where(lax.div(tile_ref[other, 0], 2) == group, 1, 0),
            0,
        )
        row = group * CAP + order
        for k in range(4):
            for side in range(2):
                send[k * 2 + side, pl.ds(row, 8, stride=16), :] = rolled[
                    side, pl.ds(k, 8, stride=4), :
                ]
        meta = jnp.where(lane == 0, 1 + lax.rem(tile, 2), 0)
        meta = jnp.where(lane == 1, lax.div(anchor_v, SUB), meta)
        meta = jnp.where(lane == 2, shift_v - 4 * sub8, meta)
        meta = jnp.where(lane == 3, lax.div(anchor_u, SUB), meta)
        meta = jnp.where(lane == 4, shift_u, meta)
        send[8, pl.ds(row, 8, stride=16), :] = meta.astype(F32)
        return carry

    lax.fori_loop(0, BLK, one_block, 0)
    for part in range(WIDE // 128):
        out_ref[:, part * 128 : part * 128 + 128] = send[part].astype(BF)


def place_kernel(recv_ref, out_ref):
    meta = recv_ref[:, FLAT:WIDE].astype(F32)
    kind, row_y, edge_v, row_x, edge_u = [
        meta[:, k : k + 1].astype(I32) for k in range(5)
    ]
    data = recv_ref[:, :FLAT].astype(F32)
    spot = lax.broadcasted_iota(I32, (PIECES, FLAT), 1)
    late_v = lax.shift_right_logical(spot, 8) < edge_v
    late_u = lax.bitwise_and(spot, 255) < edge_u
    target = lax.broadcasted_iota(I32, (PIECES, PIECES), 1)
    first = jnp.where(kind > 0, row_y * 16 + (kind - 1) * 8 + row_x, -64)
    picks, pieces = [], []
    for down in range(2):
        for right in range(2):
            keep_v = late_v if down else jnp.logical_not(late_v)
            keep_u = late_u if right else jnp.logical_not(late_u)
            pieces.append(jnp.where(keep_v & keep_u, data, 0.0).astype(BF))
            picks.append(
                jnp.where(target == first + (16 * down + right), 1.0, 0.0)
            )
    pick = jnp.concatenate(picks, axis=0)
    piece = jnp.concatenate(pieces, axis=0)
    pick = jnp.transpose(pick).astype(BF)
    out_ref[...] = jnp.dot(pick, piece, preferred_element_type=F32).astype(BF)


def total_kernel(recv_ref, out_ref):
    total = recv_ref[0:16, :].astype(F32)
    for source in range(1, 8):
        total = total + recv_ref[source * 16 : source * 16 + 16, :].astype(F32)
    for tile in range(2):
        for across in range(8):
            for k in range(4):
                row = tile * 8 + across
                out_ref[tile, k : k + 1, across * 256 : across * 256 + 256] = total[
                    row : row + 1, k * 256 : k * 256 + 256
                ]


def call(kernel, shape, dtype, spaces, scratch=(), flops=0, moved=0):
    specs = [pl.BlockSpec(memory_space=space) for space in spaces]
    return pl.pallas_call(
        kernel,
        out_shape=jax.ShapeDtypeStruct(shape, dtype),
        in_specs=specs,
        out_specs=pl.BlockSpec(memory_space=pltpu.VMEM),
        scratch_shapes=list(scratch),
        compiler_params=pltpu.CompilerParams(vmem_limit_bytes=VMEM_BYTES),
        cost_estimate=pl.CostEstimate(flops=flops, bytes_accessed=moved, transcendentals=0),
    )


def on_device(
    vis_data,
    u_cell,
    v_cell,
    u_frac,
    v_frac,
    w_plane,
    block_route,
    kernel_taps,
    taper_gain,
    sub_tile,
    sub_anchor,
):
    vm, sm = pltpu.VMEM, pltpu.SMEM
    total_slots = N_VIS * SLOTS
    packed = call(
        pack_kernel, (total_slots, COLS), BF, [vm] * 7, flops=1 << 30, moved=2 << 20
    )(block_route.reshape(1, ROWS), vis_data, u_cell, v_cell, u_frac, v_frac, w_plane)
    rows = lax.all_to_all(
        packed.reshape(N_VIS, SLOTS, COLS), VIS, split_axis=0, concat_axis=0, tiled=True
    ).reshape(total_slots, COLS)

    taps = jnp.zeros((8, 128), F32).at[:TAPS].set(kernel_taps.T.astype(BF).astype(F32))
    taper = jnp.repeat(taper_gain, POLC, axis=1)
    pieces = call(
        grid_kernel,
        (PIECES, WIDE),
        BF,
        [sm, sm, vm, vm, vm],
        scratch=[
            pltpu.VMEM((2, total_slots, 128), F32),
            pltpu.VMEM((COLS, COLS), F32),
            pltpu.VMEM((6, CHR, N_VIS * CAP), I32),
            pltpu.VMEM((2, SUB, 128), F32),
            pltpu.VMEM((WIDE // 128, PIECES, 128), F32),
        ],
        flops=1 << 32,
        moved=2 << 20,
    )(sub_tile, sub_anchor, rows, taps, taper)
    pieces = lax.all_to_all(
        pieces.reshape(32, CAP, WIDE),
        ("zl", "core", "tile"),
        split_axis=0,
        concat_axis=0,
        tiled=True,
    ).reshape(PIECES, WIDE)
    canvas = call(place_kernel, (PIECES, FLAT), BF, [vm], flops=1 << 27, moved=1 << 19)(pieces)
    canvas = lax.all_to_all(
        canvas.reshape(8, 16, FLAT), ("x", "zh"), split_axis=0, concat_axis=0, tiled=True
    ).reshape(PIECES, FLAT)
    return call(total_kernel, (2, 4, 2048), F32, [vm], moved=1 << 19)(canvas)


def solution(mesh):
    split = Mesh(
        mesh.devices.reshape(4, 2, 4, 2, 4), ("x", "zh", "zl", "core", "tile")
    )
    every = VIS + ("tile",)
    placed = (
        (P(every, None),)
        + (P(None, every),) * 5
        + (P(every, None), P(), P(), P(every, None), P(every, None))
    )
    return jax.shard_map(
        on_device, mesh=split, in_specs=placed, out_specs=P("tile", VIS, None), check_vma=False
    )
```

```python
import jax
import jax.numpy as jnp
from jax import lax
from jax.experimental import pallas as pl
from jax.experimental.pallas import tpu as pltpu
from jax.sharding import Mesh
from jax.sharding import PartitionSpec as P

ROWS = 1024
BLK = 8
SUB = 32
CHR = 16
POLC = 8
TAPS = 7
OS = 16
CAP = 4
N_VIS = 64
WIRE = 7 * BLK
DATA = CHR * POLC
PIECES = 128
FLAT = 4 * 256
WIDE = FLAT + 128
VIS = ("x", "zh", "zl", "core")
BF = jnp.bfloat16
F32 = jnp.float32
I32 = jnp.int32
VMEM_BYTES = 48 * 1024 * 1024


def pack_kernel(
    route_hbm, vis_hbm, uc_hbm, vc_hbm, uf_hbm, vf_hbm, w_hbm, out_ref, route_ref, vis_ref, code_ref, sems
):
    pairs = [(route_hbm, route_ref), (vis_hbm, vis_ref)]
    pairs += [
        (ref, code_ref.at[kind])
        for kind, ref in enumerate((uc_hbm, vc_hbm, uf_hbm, vf_hbm, w_hbm))
    ]
    copies = [
        pltpu.make_async_copy(source, target, sems.at[index])
        for index, (source, target) in enumerate(pairs)
    ]
    for copy in copies:
        copy.start()
    copies[0].wait()

    route = route_ref[...]
    route_f = route.astype(F32)
    column = jnp.transpose(jnp.broadcast_to(route_f, (8, ROWS)))[:, 0:1]
    parts = ROWS // 128
    before = lax.broadcasted_iota(I32, (128, 128), 0) < lax.broadcasted_iota(I32, (128, 128), 1)
    counts = [jnp.zeros((8, 128), F32) for _ in range(parts)]
    for first in range(parts):
        mine = jnp.broadcast_to(column[first * 128 : first * 128 + 128], (128, 128))
        for second in range(first, parts):
            same = mine == route_f[:, second * 128 : second * 128 + 128]
            if first == second:
                same = same & before
            same = jnp.where(same, 1.0, 0.0)
            counts[second] = counts[second] + jnp.sum(same.reshape(16, 8, 128), axis=0)
    rank = jnp.concatenate([jnp.sum(c, axis=0, keepdims=True) for c in counts], axis=1)
    rank_column = jnp.transpose(jnp.broadcast_to(rank, (8, ROWS)))[:, 0:1]
    rank_wide = jnp.broadcast_to(rank_column, (ROWS, 128)).astype(BF)

    for copy in copies[1:]:
        copy.wait()
    vis = vis_ref[...]
    data = jnp.concatenate(
        [jnp.where(rank_wide == jnp.asarray(r, BF), vis, jnp.zeros_like(vis)) for r in range(CAP)],
        axis=1,
    )
    codes = []
    for kind in range(5):
        values = code_ref[kind].astype(F32)
        codes += [jnp.where(rank == r, values, 0.0) for r in range(CAP)]
    codes.append(jnp.zeros((3 * 128 - 5 * CAP * CHR, ROWS), F32))
    codes = jnp.concatenate(codes, axis=0).astype(BF)

    chunk = 128
    for start in range(0, N_VIS * BLK, chunk):
        place = lax.broadcasted_iota(I32, (chunk, ROWS), 0) + start
        onehot = jnp.where(place == route, 1.0, 0.0).astype(BF)
        left = jnp.dot(onehot, data, preferred_element_type=F32)
        right = lax.dot_general(
            onehot, codes, (((1,), (1,)), ((), ())), preferred_element_type=F32
        )
        tiles = [left[:, t * 128 : t * 128 + 128] for t in range(4)]
        tiles += [right[:, t * 128 : t * 128 + 128] for t in range(3)]
        for pair in range(chunk // 16):
            packed = [
                tiles[t][row * 8 : row * 8 + 8]
                for row in (2 * pair, 2 * pair + 1)
                for t in range(7)
            ]
            at = (start // 16 + pair) * 2 * WIRE
            out_ref[at : at + 2 * WIRE, :] = jnp.concatenate(packed, axis=0).astype(BF)


def grid_kernel(
    tile_ref, anchor_ref, recv_ref, taps_ref, taper_ref, out_ref, wide, turned, codes, rolled, send
):
    wide[...] = recv_ref[...].astype(F32)
    send[...] = jnp.zeros_like(send)
    taps = taps_ref[...]
    lane = lax.broadcasted_iota(I32, (8, 128), 1)
    sub8 = lax.broadcasted_iota(I32, (8, 128), 0)
    rows16 = lax.broadcasted_iota(I32, (16, 128), 0)
    low_lanes = lax.broadcasted_iota(I32, (SUB, 128), 1) < 64
    pair_of = [
        (2 * pair + jnp.where(rows16 < 8, 0, 1)).astype(F32).astype(BF) for pair in range(4)
    ]
    zero16 = jnp.zeros((16, 128), BF)

    def weights(cell_low, index):
        picked = jnp.take_along_axis(taps, jnp.broadcast_to(index, (8, 128)), axis=1)
        return jnp.take_along_axis(picked, (sub8 - cell_low) & 7, axis=0)

    def one_block(block, carry):
        def strip(part):
            return wide[pl.ds(part * BLK + block, N_VIS, stride=WIRE), :]

        turned[...] = jnp.transpose(jnp.concatenate([strip(r) for r in range(CAP)], axis=0))
        ahead = jnp.transpose(jnp.concatenate([strip(4), strip(5)], axis=0))
        behind = jnp.transpose(jnp.concatenate([strip(6), strip(6)], axis=0))
        swapped = pltpu.roll(ahead, 64, 1)

        def kind_of(left, right, base):
            return jnp.concatenate(
                [
                    jnp.where(
                        low_lanes[:CHR],
                        left[base + r * CHR : base + r * CHR + CHR],
                        right[base + r * CHR + CHR : base + r * CHR + 2 * CHR],
                    )
                    for r in (0, 2)
                ],
                axis=1,
            ).astype(I32)

        u_cell = kind_of(ahead, swapped, 0)
        v_cell = kind_of(ahead, swapped, 64)
        u_frac = kind_of(swapped, ahead, 0)
        v_frac = kind_of(swapped, ahead, 64)
        plane = kind_of(behind, behind, 0)
        codes[0] = u_cell & 7
        codes[1] = lax.shift_right_logical(u_cell, 3)
        codes[2] = v_cell & 7
        codes[3] = lax.shift_right_logical(v_cell, 3)
        codes[4] = plane * OS + u_frac
        codes[5] = plane * OS + v_frac

        total = jnp.zeros((128, 128), F32)
        for h in range(CHR):
            a_halves, b_halves = [], []
            for half in range(2):
                at = slice(half * 128, half * 128 + 128)
                u_low, u_high, v_low, v_high, u_index, v_index = [
                    jnp.broadcast_to(codes[kind, h : h + 1, at], (8, 128)) for kind in range(6)
                ]
                turn_u = weights(u_low, u_index)
                turn_v = weights(v_low, v_index)
                samples = turned[h * POLC : (h + 1) * POLC, at]
                group_v = v_high + jnp.where(sub8 < v_low, 1, 0)
                weight_v = [jnp.where(group_v == g, turn_v, 0.0) for g in range(4)]
                weight_v = [
                    jnp.concatenate(weight_v[2 * g : 2 * g + 2], axis=0).astype(BF)
                    for g in range(2)
                ]
                high = u_high.astype(F32)
                high = jnp.concatenate([high, high], axis=0).astype(BF)
                b_rows = []
                for g in range(4):
                    mask = high == jnp.asarray(g, BF)
                    b_rows += [jnp.where(mask, part, zero16) for part in weight_v]
                b_halves.append(jnp.concatenate(b_rows, axis=0))
                low = u_low.astype(F32)
                low = jnp.concatenate([low, low], axis=0).astype(BF)
                same, later = [], []
                for pair in range(4):
                    product = [
                        jnp.broadcast_to(turn_u[s : s + 1], (8, 128)) * samples
                        for s in (2 * pair, 2 * pair + 1)
                    ]
                    product = jnp.concatenate(product, axis=0).astype(BF)
                    mask = low <= pair_of[pair]
                    same.append(jnp.where(mask, product, zero16))
                    later.append(jnp.where(mask, zero16, product))
                a_halves.append(jnp.concatenate(same + later, axis=0))
            total = total + lax.dot_general(
                jnp.concatenate(b_halves, axis=1),
                jnp.concatenate(a_halves, axis=1),
                (((1,), (1,)), ((), ())),
                preferred_element_type=F32,
            )

        crossed = pltpu.roll(total, 64, 1)
        anchor_v, anchor_u = anchor_ref[block, 0], anchor_ref[block, 1]
        shift_v = lax.rem(anchor_v, SUB)
        shift_u = lax.rem(anchor_u, SUB) * POLC
        sides = []
        for side in range(2):
            before = crossed[32:64] if side else jnp.zeros((SUB, 128), F32)
            after = crossed[96:128] if side else crossed[32:64]
            sides.append(total[side * 64 : side * 64 + 32] + jnp.where(low_lanes, before, after))
        grid = jnp.concatenate(sides, axis=1) * taper_ref[...]
        grid = pltpu.roll(grid, shift_v, 0)
        grid = pltpu.roll(grid, shift_u, 1)
        for side in range(2):
            rolled[side] = grid[:, side * 128 : side * 128 + 128]
        tile = tile_ref[block, 0]
        group = lax.div(tile, 2)
        order = lax.fori_loop(
            0,
            block,
            lambda other, n: n + jnp.where(lax.div(tile_ref[other, 0], 2) == group, 1, 0),
            0,
        )
        row = group * CAP + order
        for k in range(4):
            for side in range(2):
                send[k * 2 + side, pl.ds(row, 8, stride=16), :] = rolled[
                    side, pl.ds(k, 8, stride=4), :
                ]
        meta = jnp.where(lane == 0, 1 + lax.rem(tile, 2), 0)
        meta = jnp.where(lane == 1, lax.div(anchor_v, SUB), meta)
        meta = jnp.where(lane == 2, shift_v - 4 * sub8, meta)
        meta = jnp.where(lane == 3, lax.div(anchor_u, SUB), meta)
        meta = jnp.where(lane == 4, shift_u, meta)
        send[8, pl.ds(row, 8, stride=16), :] = meta.astype(F32)
        return carry

    lax.fori_loop(0, BLK, one_block, 0)
    for part in range(WIDE // 128):
        out_ref[:, part * 128 : part * 128 + 128] = send[part].astype(BF)


def place_kernel(recv_ref, out_ref):
    meta = recv_ref[:, FLAT:WIDE].astype(F32)
    kind, row_y, edge_v, row_x, edge_u = [
        meta[:, k : k + 1].astype(I32) for k in range(5)
    ]
    data = recv_ref[:, :FLAT].astype(F32)
    spot = lax.broadcasted_iota(I32, (PIECES, FLAT), 1)
    late_v = lax.shift_right_logical(spot, 8) < edge_v
    late_u = lax.bitwise_and(spot, 255) < edge_u
    target = lax.broadcasted_iota(I32, (PIECES, PIECES), 1)
    first = jnp.where(kind > 0, row_y * 16 + (kind - 1) * 8 + row_x, -64)
    picks, pieces = [], []
    for down in range(2):
        for right in range(2):
            keep_v = late_v if down else jnp.logical_not(late_v)
            keep_u = late_u if right else jnp.logical_not(late_u)
            pieces.append(jnp.where(keep_v & keep_u, data, 0.0).astype(BF))
            picks.append(
                jnp.where(target == first + (16 * down + right), 1.0, 0.0)
            )
    pick = jnp.concatenate(picks, axis=0)
    piece = jnp.concatenate(pieces, axis=0)
    pick = jnp.transpose(pick).astype(BF)
    out_ref[...] = jnp.dot(pick, piece, preferred_element_type=F32).astype(BF)


def total_kernel(recv_ref, out_ref):
    total = recv_ref[0:16, :].astype(F32)
    for source in range(1, 8):
        total = total + recv_ref[source * 16 : source * 16 + 16, :].astype(F32)
    for tile in range(2):
        for across in range(8):
            for k in range(4):
                row = tile * 8 + across
                out_ref[tile, k : k + 1, across * 256 : across * 256 + 256] = total[
                    row : row + 1, k * 256 : k * 256 + 256
                ]


def call(kernel, shape, dtype, spaces, scratch=(), flops=0, moved=0):
    specs = [pl.BlockSpec(memory_space=space) for space in spaces]
    return pl.pallas_call(
        kernel,
        out_shape=jax.ShapeDtypeStruct(shape, dtype),
        in_specs=specs,
        out_specs=pl.BlockSpec(memory_space=pltpu.VMEM),
        scratch_shapes=list(scratch),
        compiler_params=pltpu.CompilerParams(vmem_limit_bytes=VMEM_BYTES),
        cost_estimate=pl.CostEstimate(flops=flops, bytes_accessed=moved, transcendentals=0),
    )


def on_device(
    vis_data,
    u_cell,
    v_cell,
    u_frac,
    v_frac,
    w_plane,
    block_route,
    kernel_taps,
    taper_gain,
    sub_tile,
    sub_anchor,
):
    vm, sm, hbm = pltpu.VMEM, pltpu.SMEM, pltpu.HBM
    packed = call(
        pack_kernel,
        (N_VIS * WIRE, 128),
        BF,
        [hbm] * 7,
        scratch=[
            pltpu.VMEM((1, ROWS), I32),
            pltpu.VMEM((ROWS, DATA), BF),
            pltpu.VMEM((5, CHR, ROWS), I32),
            pltpu.SemaphoreType.DMA((7,)),
        ],
        flops=1 << 30,
        moved=2 << 20,
    )(block_route.reshape(1, ROWS), vis_data, u_cell, v_cell, u_frac, v_frac, w_plane)
    rows = lax.all_to_all(
        packed.reshape(N_VIS, WIRE, 128), VIS, split_axis=0, concat_axis=0, tiled=True
    ).reshape(N_VIS * WIRE, 128)

    taps = jnp.zeros((8, 128), F32).at[:TAPS].set(kernel_taps.T.astype(BF).astype(F32))
    taper = jnp.repeat(taper_gain, POLC, axis=1)
    pieces = call(
        grid_kernel,
        (PIECES, WIDE),
        BF,
        [sm, sm, vm, vm, vm],
        scratch=[
            pltpu.VMEM((N_VIS * WIRE, 128), F32),
            pltpu.VMEM((DATA, N_VIS * CAP), F32),
            pltpu.VMEM((6, CHR, N_VIS * CAP), I32),
            pltpu.VMEM((2, SUB, 128), F32),
            pltpu.VMEM((WIDE // 128, PIECES, 128), F32),
        ],
        flops=1 << 32,
        moved=2 << 20,
    )(sub_tile, sub_anchor, rows, taps, taper)
    pieces = lax.all_to_all(
        pieces.reshape(32, CAP, WIDE),
        ("zl", "core", "tile"),
        split_axis=0,
        concat_axis=0,
        tiled=True,
    ).reshape(PIECES, WIDE)
    canvas = call(place_kernel, (PIECES, FLAT), BF, [vm], flops=1 << 27, moved=1 << 19)(pieces)
    canvas = lax.all_to_all(
        canvas.reshape(8, 16, FLAT), ("x", "zh"), split_axis=0, concat_axis=0, tiled=True
    ).reshape(PIECES, FLAT)
    return call(total_kernel, (2, 4, 2048), F32, [vm], moved=1 << 19)(canvas)


def solution(mesh):
    split = Mesh(
        mesh.devices.reshape(4, 2, 4, 2, 4), ("x", "zh", "zl", "core", "tile")
    )
    every = VIS + ("tile",)
    placed = (
        (P(every, None),)
        + (P(None, every),) * 5
        + (P(every, None), P(), P(), P(every, None), P(every, None))
    )
    return jax.shard_map(
        on_device, mesh=split, in_specs=placed, out_specs=P("tile", VIS, None), check_vma=False
    )
```

```python
import jax
import jax.numpy as jnp
from jax import lax
from jax.experimental import pallas as pl
from jax.experimental.pallas import tpu as pltpu
from jax.sharding import Mesh
from jax.sharding import PartitionSpec as P

ROWS = 1024
BLK = 8
SUB = 32
CHR = 16
POLC = 8
TAPS = 7
OS = 16
CAP = 4
N_VIS = 64
WIRE = 7 * BLK
DATA = CHR * POLC
PIECES = 128
FLAT = 4 * 256
WIDE = FLAT + 128
VIS = ("x", "zh", "zl", "core")
BF = jnp.bfloat16
F32 = jnp.float32
I32 = jnp.int32
VMEM_BYTES = 48 * 1024 * 1024


def pack_kernel(
    route_hbm, vis_hbm, uc_hbm, vc_hbm, uf_hbm, vf_hbm, w_hbm, out_hbm, route_ref, vis_ref, code_ref, line_ref, sems
):
    pairs = [(route_hbm, route_ref), (vis_hbm, vis_ref)]
    pairs += [
        (ref, code_ref.at[kind])
        for kind, ref in enumerate((uc_hbm, vc_hbm, uf_hbm, vf_hbm, w_hbm))
    ]
    copies = [
        pltpu.make_async_copy(source, target, sems.at[index])
        for index, (source, target) in enumerate(pairs)
    ]
    for copy in copies:
        copy.start()
    copies[0].wait()

    route = route_ref[...]
    route_f = route.astype(F32)
    column = jnp.transpose(jnp.broadcast_to(route_f, (8, ROWS)))[:, 0:1]
    parts = ROWS // 128
    before = lax.broadcasted_iota(I32, (128, 128), 0) < lax.broadcasted_iota(I32, (128, 128), 1)
    counts = [jnp.zeros((8, 128), F32) for _ in range(parts)]
    for first in range(parts):
        mine = jnp.broadcast_to(column[first * 128 : first * 128 + 128], (128, 128))
        for second in range(first, parts):
            same = mine == route_f[:, second * 128 : second * 128 + 128]
            if first == second:
                same = same & before
            same = jnp.where(same, 1.0, 0.0)
            counts[second] = counts[second] + jnp.sum(same.reshape(16, 8, 128), axis=0)
    rank = jnp.concatenate([jnp.sum(c, axis=0, keepdims=True) for c in counts], axis=1)
    rank_column = jnp.transpose(jnp.broadcast_to(rank, (8, ROWS)))[:, 0:1]
    rank_wide = jnp.broadcast_to(rank_column, (ROWS, 128)).astype(BF)

    for copy in copies[1:]:
        copy.wait()
    vis = vis_ref[...]
    data = jnp.concatenate(
        [jnp.where(rank_wide == jnp.asarray(r, BF), vis, jnp.zeros_like(vis)) for r in range(CAP)],
        axis=1,
    )
    codes = []
    for kind in range(5):
        values = code_ref[kind].astype(F32)
        codes += [jnp.where(rank == r, values, 0.0) for r in range(CAP)]
    codes.append(jnp.zeros((3 * 128 - 5 * CAP * CHR, ROWS), F32))
    codes = jnp.concatenate(codes, axis=0).astype(BF)

    chunk = N_VIS * BLK // PACK_PARTS
    leaving = []
    for start in range(0, N_VIS * BLK, chunk):
        place = lax.broadcasted_iota(I32, (chunk, ROWS), 0) + start
        onehot = jnp.where(place == route, 1.0, 0.0).astype(BF)
        left = jnp.dot(onehot, data, preferred_element_type=F32)
        right = lax.dot_general(
            onehot, codes, (((1,), (1,)), ((), ())), preferred_element_type=F32
        )
        tiles = [left[:, t * 128 : t * 128 + 128] for t in range(4)]
        tiles += [right[:, t * 128 : t * 128 + 128] for t in range(3)]
        for pair in range(chunk // 16):
            packed = [
                tiles[t][row * 8 : row * 8 + 8]
                for row in (2 * pair, 2 * pair + 1)
                for t in range(7)
            ]
            at = (start // 16 + pair) * 2 * WIRE
            line_ref[at : at + 2 * WIRE, :] = jnp.concatenate(packed, axis=0).astype(BF)
        lines = pl.ds(start // BLK * WIRE, chunk // BLK * WIRE)
        leaving.append(
            pltpu.make_async_copy(
                line_ref.at[lines, :], out_hbm.at[lines, :], sems.at[7 + start // chunk]
            )
        )
        leaving[-1].start()
    for copy in leaving:
        copy.wait()


def grid_kernel(
    tile_ref, anchor_ref, recv_ref, taps_ref, taper_ref, out_ref, wide, turned, codes, sums, rolled, send
):
    wide[...] = recv_ref[...].astype(F32)
    send[...] = jnp.zeros_like(send)
    taps = taps_ref[...]
    lane = lax.broadcasted_iota(I32, (8, 128), 1)
    sub8 = lax.broadcasted_iota(I32, (8, 128), 0)
    rows16 = lax.broadcasted_iota(I32, (16, 128), 0)
    low_lanes = lax.broadcasted_iota(I32, (SUB, 128), 1) < 64
    pair_of = [
        (2 * pair + jnp.where(rows16 < 8, 0, 1)).astype(F32).astype(BF) for pair in range(4)
    ]
    zero16 = jnp.zeros((16, 128), BF)

    def weights(cell_low, index):
        picked = jnp.take_along_axis(taps, jnp.broadcast_to(index, (8, 128)), axis=1)
        return jnp.take_along_axis(picked, (sub8 - cell_low) & 7, axis=0)

    for block in range(BLK):

        def strip(part):
            return wide[pl.ds(part * BLK + block, N_VIS, stride=WIRE), :]

        turned[block] = jnp.transpose(jnp.concatenate([strip(r) for r in range(CAP)], axis=0))
        ahead = jnp.transpose(jnp.concatenate([strip(4), strip(5)], axis=0))
        behind = jnp.transpose(jnp.concatenate([strip(6), strip(6)], axis=0))
        swapped = pltpu.roll(ahead, 64, 1)

        def kind_of(left, right, base):
            return jnp.concatenate(
                [
                    jnp.where(
                        low_lanes[:CHR],
                        left[base + r * CHR : base + r * CHR + CHR],
                        right[base + r * CHR + CHR : base + r * CHR + 2 * CHR],
                    )
                    for r in (0, 2)
                ],
                axis=1,
            ).astype(I32)

        u_cell = kind_of(ahead, swapped, 0)
        v_cell = kind_of(ahead, swapped, 64)
        u_frac = kind_of(swapped, ahead, 0)
        v_frac = kind_of(swapped, ahead, 64)
        plane = kind_of(behind, behind, 0)
        codes[block, 0] = u_cell & 7
        codes[block, 1] = lax.shift_right_logical(u_cell, 3)
        codes[block, 2] = v_cell & 7
        codes[block, 3] = lax.shift_right_logical(v_cell, 3)
        codes[block, 4] = plane * OS + u_frac
        codes[block, 5] = plane * OS + v_frac

    def one_block(block, carry):
        total = jnp.zeros((128, 128), F32)
        for h in range(CHR):
            a_halves, b_halves = [], []
            for half in range(2):
                at = slice(half * 128, half * 128 + 128)
                u_low, u_high, v_low, v_high, u_index, v_index = [
                    jnp.broadcast_to(codes[block, kind, h : h + 1, at], (8, 128))
                    for kind in range(6)
                ]
                turn_u = weights(u_low, u_index)
                turn_v = weights(v_low, v_index)
                samples = turned[block, h * POLC : (h + 1) * POLC, at]
                group_v = v_high + jnp.where(sub8 < v_low, 1, 0)
                weight_v = [jnp.where(group_v == g, turn_v, 0.0) for g in range(4)]
                weight_v = [
                    jnp.concatenate(weight_v[2 * g : 2 * g + 2], axis=0).astype(BF)
                    for g in range(2)
                ]
                high = u_high.astype(F32)
                high = jnp.concatenate([high, high], axis=0).astype(BF)
                b_rows = []
                for g in range(4):
                    mask = high == jnp.asarray(g, BF)
                    b_rows += [jnp.where(mask, part, zero16) for part in weight_v]
                b_halves.append(jnp.concatenate(b_rows, axis=0))
                low = u_low.astype(F32)
                low = jnp.concatenate([low, low], axis=0).astype(BF)
                same, later = [], []
                for pair in range(4):
                    product = [
                        jnp.broadcast_to(turn_u[s : s + 1], (8, 128)) * samples
                        for s in (2 * pair, 2 * pair + 1)
                    ]
                    product = jnp.concatenate(product, axis=0).astype(BF)
                    mask = low <= pair_of[pair]
                    same.append(jnp.where(mask, product, zero16))
                    later.append(jnp.where(mask, zero16, product))
                a_halves.append(jnp.concatenate(same + later, axis=0))
            total = total + lax.dot_general(
                jnp.concatenate(b_halves, axis=1),
                jnp.concatenate(a_halves, axis=1),
                (((1,), (1,)), ((), ())),
                preferred_element_type=F32,
            )
        sums[block] = total
        return carry

    lax.fori_loop(0, BLK, one_block, 0)

    taper = taper_ref[...]
    tiles = [tile_ref[block, 0] for block in range(BLK)]
    groups = [lax.div(tile, 2) for tile in tiles]
    for block in range(BLK):
        total = sums[block]
        crossed = pltpu.roll(total, 64, 1)
        anchor_v, anchor_u = anchor_ref[block, 0], anchor_ref[block, 1]
        shift_v = lax.rem(anchor_v, SUB)
        shift_u = lax.rem(anchor_u, SUB) * POLC
        sides = []
        for side in range(2):
            before = crossed[32:64] if side else jnp.zeros((SUB, 128), F32)
            after = crossed[96:128] if side else crossed[32:64]
            sides.append(total[side * 64 : side * 64 + 32] + jnp.where(low_lanes, before, after))
        grid = jnp.concatenate(sides, axis=1) * taper
        grid = pltpu.roll(grid, shift_v, 0)
        grid = pltpu.roll(grid, shift_u, 1)
        for side in range(2):
            rolled[block, side] = grid[:, side * 128 : side * 128 + 128]
        order = jnp.int32(0)
        for other in range(block):
            order = order + jnp.where(groups[other] == groups[block], 1, 0)
        row = groups[block] * CAP + order
        for k in range(4):
            for side in range(2):
                send[k * 2 + side, pl.ds(row, 8, stride=16), :] = rolled[
                    block, side, pl.ds(k, 8, stride=4), :
                ]
        meta = jnp.where(lane == 0, 1 + lax.rem(tiles[block], 2), 0)
        meta = jnp.where(lane == 1, lax.div(anchor_v, SUB), meta)
        meta = jnp.where(lane == 2, shift_v - 4 * sub8, meta)
        meta = jnp.where(lane == 3, lax.div(anchor_u, SUB), meta)
        meta = jnp.where(lane == 4, shift_u, meta)
        send[8, pl.ds(row, 8, stride=16), :] = meta.astype(F32)
    for part in range(WIDE // 128):
        out_ref[:, part * 128 : part * 128 + 128] = send[part].astype(BF)


def place_kernel(recv_ref, out_ref):
    meta = recv_ref[:, FLAT:WIDE].astype(F32)
    kind, row_y, edge_v, row_x, edge_u = [
        meta[:, k : k + 1].astype(I32) for k in range(5)
    ]
    data = recv_ref[:, :FLAT].astype(F32)
    spot = lax.broadcasted_iota(I32, (PIECES, FLAT), 1)
    late_v = lax.shift_right_logical(spot, 8) < edge_v
    late_u = lax.bitwise_and(spot, 255) < edge_u
    target = lax.broadcasted_iota(I32, (PIECES, PIECES), 1)
    first = jnp.where(kind > 0, row_y * 16 + (kind - 1) * 8 + row_x, -64)
    picks, pieces = [], []
    for down in range(2):
        for right in range(2):
            keep_v = late_v if down else jnp.logical_not(late_v)
            keep_u = late_u if right else jnp.logical_not(late_u)
            pieces.append(jnp.where(keep_v & keep_u, data, 0.0).astype(BF))
            picks.append(
                jnp.where(target == first + (16 * down + right), 1.0, 0.0)
            )
    pick = jnp.concatenate(picks, axis=0)
    piece = jnp.concatenate(pieces, axis=0)
    pick = jnp.transpose(pick).astype(BF)
    out_ref[...] = jnp.dot(pick, piece, preferred_element_type=F32).astype(BF)


def total_kernel(recv_ref, out_ref):
    total = recv_ref[0:16, :].astype(F32)
    for source in range(1, 8):
        total = total + recv_ref[source * 16 : source * 16 + 16, :].astype(F32)
    for tile in range(2):
        for across in range(8):
            for k in range(4):
                row = tile * 8 + across
                out_ref[tile, k : k + 1, across * 256 : across * 256 + 256] = total[
                    row : row + 1, k * 256 : k * 256 + 256
                ]


PACK_PARTS = 4
PACK_BYTES = None
PACK_SCRATCH = [
    pltpu.VMEM((1, ROWS), I32),
    pltpu.VMEM((ROWS, DATA), BF),
    pltpu.VMEM((5, CHR, ROWS), I32),
    pltpu.VMEM((N_VIS * WIRE, 128), BF),
    pltpu.SemaphoreType.DMA((7 + PACK_PARTS,)),
]
GRID_SCRATCH = [
    pltpu.VMEM((N_VIS * WIRE, 128), F32),
    pltpu.VMEM((BLK, DATA, N_VIS * CAP), F32),
    pltpu.VMEM((BLK, 6, CHR, N_VIS * CAP), I32),
    pltpu.VMEM((BLK, 128, 128), F32),
    pltpu.VMEM((BLK, 2, SUB, 128), F32),
    pltpu.VMEM((WIDE // 128, PIECES, 128), F32),
]


def call(
    kernel, shape, dtype, spaces, scratch=(), flops=0, moved=0, out=pltpu.VMEM, limit=VMEM_BYTES
):
    specs = [pl.BlockSpec(memory_space=space) for space in spaces]
    return pl.pallas_call(
        kernel,
        out_shape=jax.ShapeDtypeStruct(shape, dtype),
        in_specs=specs,
        out_specs=pl.BlockSpec(memory_space=out),
        scratch_shapes=list(scratch),
        compiler_params=pltpu.CompilerParams(vmem_limit_bytes=limit),
        cost_estimate=pl.CostEstimate(flops=flops, bytes_accessed=moved, transcendentals=0),
    )


def on_device(
    vis_data,
    u_cell,
    v_cell,
    u_frac,
    v_frac,
    w_plane,
    block_route,
    kernel_taps,
    taper_gain,
    sub_tile,
    sub_anchor,
):
    vm, sm, hbm = pltpu.VMEM, pltpu.SMEM, pltpu.HBM
    packed = call(
        pack_kernel,
        (N_VIS * WIRE, 128),
        BF,
        [hbm] * 7,
        scratch=PACK_SCRATCH,
        flops=1 << 30,
        moved=2 << 20,
        out=hbm,
        limit=PACK_BYTES,
    )(block_route.reshape(1, ROWS), vis_data, u_cell, v_cell, u_frac, v_frac, w_plane)
    rows = lax.all_to_all(
        packed.reshape(N_VIS, WIRE, 128), VIS, split_axis=0, concat_axis=0, tiled=True
    ).reshape(N_VIS * WIRE, 128)

    taps = jnp.zeros((8, 128), F32).at[:TAPS].set(kernel_taps.T.astype(BF).astype(F32))
    taper = jnp.repeat(taper_gain, POLC, axis=1)
    pieces = call(
        grid_kernel,
        (PIECES, WIDE),
        BF,
        [sm, sm, vm, vm, vm],
        scratch=GRID_SCRATCH,
        flops=1 << 32,
        moved=2 << 20,
    )(sub_tile, sub_anchor, rows, taps, taper)
    pieces = lax.all_to_all(
        pieces.reshape(32, CAP, WIDE),
        ("zl", "core", "tile"),
        split_axis=0,
        concat_axis=0,
        tiled=True,
    ).reshape(PIECES, WIDE)
    canvas = call(place_kernel, (PIECES, FLAT), BF, [vm], flops=1 << 27, moved=1 << 19)(pieces)
    canvas = lax.all_to_all(
        canvas.reshape(8, 16, FLAT), ("x", "zh"), split_axis=0, concat_axis=0, tiled=True
    ).reshape(PIECES, FLAT)
    return call(total_kernel, (2, 4, 2048), F32, [vm], moved=1 << 19)(canvas)


def solution(mesh):
    split = Mesh(
        mesh.devices.reshape(4, 2, 4, 2, 4), ("x", "zh", "zl", "core", "tile")
    )
    every = VIS + ("tile",)
    placed = (
        (P(every, None),)
        + (P(None, every),) * 5
        + (P(every, None), P(), P(), P(every, None), P(every, None))
    )
    return jax.shard_map(
        on_device, mesh=split, in_specs=placed, out_specs=P("tile", VIS, None), check_vma=False
    )
```

```python
import jax
import jax.numpy as jnp
from jax import lax
from jax.experimental import pallas as pl
from jax.experimental.pallas import tpu as pltpu
from jax.sharding import Mesh
from jax.sharding import PartitionSpec as P

ROWS = 1024
BLK = 8
SUB = 32
CHR = 16
POLC = 8
TAPS = 7
OS = 16
CAP = 4
N_VIS = 64
WIRE = 7 * BLK
DATA = CHR * POLC
PIECES = 128
FLAT = 4 * 256
WIDE = FLAT + 128
VIS = ("x", "zh", "zl", "core")
BF = jnp.bfloat16
F32 = jnp.float32
I32 = jnp.int32
VMEM_BYTES = 48 * 1024 * 1024


def pack_kernel(
    route_hbm, vis_hbm, uc_hbm, vc_hbm, uf_hbm, vf_hbm, w_hbm, out_hbm, route_ref, vis_ref, code_ref, line_ref, sems
):
    pairs = [(route_hbm, route_ref), (vis_hbm, vis_ref)]
    pairs += [
        (ref, code_ref.at[kind])
        for kind, ref in enumerate((uc_hbm, vc_hbm, uf_hbm, vf_hbm, w_hbm))
    ]
    copies = [
        pltpu.make_async_copy(source, target, sems.at[index])
        for index, (source, target) in enumerate(pairs)
    ]
    for copy in copies:
        copy.start()
    copies[0].wait()

    route = route_ref[...]
    route_f = route.astype(F32)
    column = jnp.transpose(jnp.broadcast_to(route_f, (8, ROWS)))[:, 0:1]
    parts = ROWS // 128
    before = lax.broadcasted_iota(I32, (128, 128), 0) < lax.broadcasted_iota(I32, (128, 128), 1)
    counts = [jnp.zeros((8, 128), F32) for _ in range(parts)]
    for first in range(parts):
        mine = jnp.broadcast_to(column[first * 128 : first * 128 + 128], (128, 128))
        for second in range(first, parts):
            same = mine == route_f[:, second * 128 : second * 128 + 128]
            if first == second:
                same = same & before
            same = jnp.where(same, 1.0, 0.0)
            counts[second] = counts[second] + jnp.sum(same.reshape(16, 8, 128), axis=0)
    rank = jnp.concatenate([jnp.sum(c, axis=0, keepdims=True) for c in counts], axis=1)
    rank_column = jnp.transpose(jnp.broadcast_to(rank, (8, ROWS)))[:, 0:1]
    rank_wide = jnp.broadcast_to(rank_column, (ROWS, 128)).astype(BF)

    for copy in copies[1:]:
        copy.wait()
    vis = vis_ref[...]
    data = jnp.concatenate(
        [jnp.where(rank_wide == jnp.asarray(r, BF), vis, jnp.zeros_like(vis)) for r in range(CAP)],
        axis=1,
    )
    codes = []
    for kind in range(5):
        values = code_ref[kind].astype(F32)
        codes += [jnp.where(rank == r, values, 0.0) for r in range(CAP)]
    codes.append(jnp.zeros((3 * 128 - 5 * CAP * CHR, ROWS), F32))
    codes = jnp.concatenate(codes, axis=0).astype(BF)

    chunk = N_VIS * BLK // PACK_PARTS
    leaving = []
    for start in range(0, N_VIS * BLK, chunk):
        place = lax.broadcasted_iota(I32, (chunk, ROWS), 0) + start
        onehot = jnp.where(place == route, 1.0, 0.0).astype(BF)
        left = jnp.dot(onehot, data, preferred_element_type=F32)
        right = lax.dot_general(
            onehot, codes, (((1,), (1,)), ((), ())), preferred_element_type=F32
        )
        tiles = [left[:, t * 128 : t * 128 + 128] for t in range(4)]
        tiles += [right[:, t * 128 : t * 128 + 128] for t in range(3)]
        for pair in range(chunk // 16):
            packed = [
                tiles[t][row * 8 : row * 8 + 8]
                for row in (2 * pair, 2 * pair + 1)
                for t in range(7)
            ]
            at = (start // 16 + pair) * 2 * WIRE
            line_ref[at : at + 2 * WIRE, :] = jnp.concatenate(packed, axis=0).astype(BF)
        lines = pl.ds(start // BLK * WIRE, chunk // BLK * WIRE)
        leaving.append(
            pltpu.make_async_copy(
                line_ref.at[lines, :], out_hbm.at[lines, :], sems.at[7 + start // chunk]
            )
        )
        leaving[-1].start()
    for copy in leaving:
        copy.wait()


def grid_kernel(
    tile_ref, anchor_ref, recv_ref, taps_ref, taper_ref, out_ref, wide, turned, codes, sums, rolled, send
):
    wide[...] = recv_ref[...].astype(F32)
    send[...] = jnp.zeros_like(send)
    taps = taps_ref[...]
    lane = lax.broadcasted_iota(I32, (8, 128), 1)
    sub8 = lax.broadcasted_iota(I32, (8, 128), 0)
    rows16 = lax.broadcasted_iota(I32, (16, 128), 0)
    low_lanes = lax.broadcasted_iota(I32, (SUB, 128), 1) < 64
    pair_of = [
        (2 * pair + jnp.where(rows16 < 8, 0, 1)).astype(F32).astype(BF) for pair in range(4)
    ]
    zero16 = jnp.zeros((16, 128), BF)

    def weights(cell_low, index):
        picked = jnp.take_along_axis(taps, jnp.broadcast_to(index, (8, 128)), axis=1)
        return jnp.take_along_axis(picked, (sub8 - cell_low) & 7, axis=0)

    for block in range(BLK):

        def strip(part):
            return wide[pl.ds(part * BLK + block, N_VIS, stride=WIRE), :]

        turned[block] = jnp.transpose(jnp.concatenate([strip(r) for r in range(CAP)], axis=0))
        ahead = jnp.transpose(jnp.concatenate([strip(4), strip(5)], axis=0))
        behind = jnp.transpose(jnp.concatenate([strip(6), strip(6)], axis=0))
        swapped = pltpu.roll(ahead, 64, 1)

        def kind_of(left, right, base):
            return jnp.concatenate(
                [
                    jnp.where(
                        low_lanes[:CHR],
                        left[base + r * CHR : base + r * CHR + CHR],
                        right[base + r * CHR + CHR : base + r * CHR + 2 * CHR],
                    )
                    for r in (0, 2)
                ],
                axis=1,
            ).astype(I32)

        u_cell = kind_of(ahead, swapped, 0)
        v_cell = kind_of(ahead, swapped, 64)
        u_frac = kind_of(swapped, ahead, 0)
        v_frac = kind_of(swapped, ahead, 64)
        plane = kind_of(behind, behind, 0)
        codes[block, 0] = u_cell & 7
        codes[block, 1] = lax.shift_right_logical(u_cell, 3)
        codes[block, 2] = v_cell & 7
        codes[block, 3] = lax.shift_right_logical(v_cell, 3)
        codes[block, 4] = plane * OS + u_frac
        codes[block, 5] = plane * OS + v_frac

    def one_block(block, carry):
        total = jnp.zeros((128, 128), F32)
        for h in range(CHR):
            a_halves, b_halves = [], []
            for half in range(2):
                at = slice(half * 128, half * 128 + 128)
                u_low, u_high, v_low, v_high, u_index, v_index = [
                    jnp.broadcast_to(codes[block, kind, h : h + 1, at], (8, 128))
                    for kind in range(6)
                ]
                turn_u = weights(u_low, u_index)
                turn_v = weights(v_low, v_index)
                samples = turned[block, h * POLC : (h + 1) * POLC, at]
                group_v = v_high + jnp.where(sub8 < v_low, 1, 0)
                weight_v = [jnp.where(group_v == g, turn_v, 0.0) for g in range(4)]
                weight_v = [
                    jnp.concatenate(weight_v[2 * g : 2 * g + 2], axis=0).astype(BF)
                    for g in range(2)
                ]
                high = u_high.astype(F32)
                high = jnp.concatenate([high, high], axis=0).astype(BF)
                b_rows = []
                for g in range(4):
                    mask = high == jnp.asarray(g, BF)
                    b_rows += [jnp.where(mask, part, zero16) for part in weight_v]
                b_halves.append(jnp.concatenate(b_rows, axis=0))
                low = u_low.astype(F32)
                low = jnp.concatenate([low, low], axis=0).astype(BF)
                same, later = [], []
                for pair in range(4):
                    product = [
                        jnp.broadcast_to(turn_u[s : s + 1], (8, 128)) * samples
                        for s in (2 * pair, 2 * pair + 1)
                    ]
                    product = jnp.concatenate(product, axis=0).astype(BF)
                    mask = low <= pair_of[pair]
                    same.append(jnp.where(mask, product, zero16))
                    later.append(jnp.where(mask, zero16, product))
                a_halves.append(jnp.concatenate(same + later, axis=0))
            total = total + lax.dot_general(
                jnp.concatenate(b_halves, axis=1),
                jnp.concatenate(a_halves, axis=1),
                (((1,), (1,)), ((), ())),
                preferred_element_type=F32,
            )
        sums[block] = total
        return carry

    lax.fori_loop(0, BLK, one_block, 0, unroll=8)

    taper = taper_ref[...]
    tiles = [tile_ref[block, 0] for block in range(BLK)]
    groups = [lax.div(tile, 2) for tile in tiles]
    for block in range(BLK):
        total = sums[block]
        crossed = pltpu.roll(total, 64, 1)
        anchor_v, anchor_u = anchor_ref[block, 0], anchor_ref[block, 1]
        shift_v = lax.rem(anchor_v, SUB)
        shift_u = lax.rem(anchor_u, SUB) * POLC
        sides = []
        for side in range(2):
            before = crossed[32:64] if side else jnp.zeros((SUB, 128), F32)
            after = crossed[96:128] if side else crossed[32:64]
            sides.append(total[side * 64 : side * 64 + 32] + jnp.where(low_lanes, before, after))
        grid = jnp.concatenate(sides, axis=1) * taper
        grid = pltpu.roll(grid, shift_v, 0)
        grid = pltpu.roll(grid, shift_u, 1)
        for side in range(2):
            rolled[block, side] = grid[:, side * 128 : side * 128 + 128]
        order = jnp.int32(0)
        for other in range(block):
            order = order + jnp.where(groups[other] == groups[block], 1, 0)
        row = groups[block] * CAP + order
        for k in range(4):
            for side in range(2):
                send[k * 2 + side, pl.ds(row, 8, stride=16), :] = rolled[
                    block, side, pl.ds(k, 8, stride=4), :
                ]
        meta = jnp.where(lane == 0, 1 + lax.rem(tiles[block], 2), 0)
        meta = jnp.where(lane == 1, lax.div(anchor_v, SUB), meta)
        meta = jnp.where(lane == 2, shift_v - 4 * sub8, meta)
        meta = jnp.where(lane == 3, lax.div(anchor_u, SUB), meta)
        meta = jnp.where(lane == 4, shift_u, meta)
        send[8, pl.ds(row, 8, stride=16), :] = meta.astype(F32)
    for part in range(WIDE // 128):
        out_ref[:, part * 128 : part * 128 + 128] = send[part].astype(BF)


def place_kernel(recv_ref, out_ref):
    meta = recv_ref[:, FLAT:WIDE].astype(F32)
    kind, row_y, edge_v, row_x, edge_u = [
        meta[:, k : k + 1].astype(I32) for k in range(5)
    ]
    data = recv_ref[:, :FLAT].astype(F32)
    spot = lax.broadcasted_iota(I32, (PIECES, FLAT), 1)
    late_v = lax.shift_right_logical(spot, 8) < edge_v
    late_u = lax.bitwise_and(spot, 255) < edge_u
    target = lax.broadcasted_iota(I32, (PIECES, PIECES), 1)
    first = jnp.where(kind > 0, row_y * 16 + (kind - 1) * 8 + row_x, -64)
    picks, pieces = [], []
    for down in range(2):
        for right in range(2):
            keep_v = late_v if down else jnp.logical_not(late_v)
            keep_u = late_u if right else jnp.logical_not(late_u)
            pieces.append(jnp.where(keep_v & keep_u, data, 0.0).astype(BF))
            picks.append(
                jnp.where(target == first + (16 * down + right), 1.0, 0.0)
            )
    pick = jnp.concatenate(picks, axis=0)
    piece = jnp.concatenate(pieces, axis=0)
    pick = jnp.transpose(pick).astype(BF)
    out_ref[...] = jnp.dot(pick, piece, preferred_element_type=F32).astype(BF)


def total_kernel(recv_ref, out_ref):
    total = recv_ref[0:16, :].astype(F32)
    for source in range(1, 8):
        total = total + recv_ref[source * 16 : source * 16 + 16, :].astype(F32)
    for tile in range(2):
        for across in range(8):
            for k in range(4):
                row = tile * 8 + across
                out_ref[tile, k : k + 1, across * 256 : across * 256 + 256] = total[
                    row : row + 1, k * 256 : k * 256 + 256
                ]


PACK_PARTS = 2
PACK_BYTES = None
PACK_SCRATCH = [
    pltpu.VMEM((1, ROWS), I32),
    pltpu.VMEM((ROWS, DATA), BF),
    pltpu.VMEM((5, CHR, ROWS), I32),
    pltpu.VMEM((N_VIS * WIRE, 128), BF),
    pltpu.SemaphoreType.DMA((7 + PACK_PARTS,)),
]
GRID_SCRATCH = [
    pltpu.VMEM((N_VIS * WIRE, 128), F32),
    pltpu.VMEM((BLK, DATA, N_VIS * CAP), F32),
    pltpu.VMEM((BLK, 6, CHR, N_VIS * CAP), I32),
    pltpu.VMEM((BLK, 128, 128), F32),
    pltpu.VMEM((BLK, 2, SUB, 128), F32),
    pltpu.VMEM((WIDE // 128, PIECES, 128), F32),
]


def call(
    kernel, shape, dtype, spaces, scratch=(), flops=0, moved=0, out=pltpu.VMEM, limit=VMEM_BYTES
):
    specs = [pl.BlockSpec(memory_space=space) for space in spaces]
    return pl.pallas_call(
        kernel,
        out_shape=jax.ShapeDtypeStruct(shape, dtype),
        in_specs=specs,
        out_specs=pl.BlockSpec(memory_space=out),
        scratch_shapes=list(scratch),
        compiler_params=pltpu.CompilerParams(vmem_limit_bytes=limit),
        cost_estimate=pl.CostEstimate(flops=flops, bytes_accessed=moved, transcendentals=0),
    )


def on_device(
    vis_data,
    u_cell,
    v_cell,
    u_frac,
    v_frac,
    w_plane,
    block_route,
    kernel_taps,
    taper_gain,
    sub_tile,
    sub_anchor,
):
    vm, sm, hbm = pltpu.VMEM, pltpu.SMEM, pltpu.HBM
    packed = call(
        pack_kernel,
        (N_VIS * WIRE, 128),
        BF,
        [hbm] * 7,
        scratch=PACK_SCRATCH,
        flops=1 << 30,
        moved=2 << 20,
        out=hbm,
        limit=PACK_BYTES,
    )(block_route.reshape(1, ROWS), vis_data, u_cell, v_cell, u_frac, v_frac, w_plane)
    rows = lax.all_to_all(
        packed.reshape(N_VIS, WIRE, 128), VIS, split_axis=0, concat_axis=0, tiled=True
    ).reshape(N_VIS * WIRE, 128)

    taps = jnp.zeros((8, 128), F32).at[:TAPS].set(kernel_taps.T.astype(BF).astype(F32))
    taper = jnp.repeat(taper_gain, POLC, axis=1)
    pieces = call(
        grid_kernel,
        (PIECES, WIDE),
        BF,
        [sm, sm, vm, vm, vm],
        scratch=GRID_SCRATCH,
        flops=1 << 32,
        moved=2 << 20,
    )(sub_tile, sub_anchor, rows, taps, taper)
    pieces = lax.all_to_all(
        pieces.reshape(32, CAP, WIDE),
        ("zl", "core", "tile"),
        split_axis=0,
        concat_axis=0,
        tiled=True,
    ).reshape(PIECES, WIDE)
    canvas = call(place_kernel, (PIECES, FLAT), BF, [vm], flops=1 << 27, moved=1 << 19)(pieces)
    canvas = lax.all_to_all(
        canvas.reshape(8, 16, FLAT), ("x", "zh"), split_axis=0, concat_axis=0, tiled=True
    ).reshape(PIECES, FLAT)
    return call(total_kernel, (2, 4, 2048), F32, [vm], moved=1 << 19)(canvas)


def solution(mesh):
    split = Mesh(
        mesh.devices.reshape(4, 2, 4, 2, 4), ("x", "zh", "zl", "core", "tile")
    )
    every = VIS + ("tile",)
    placed = (
        (P(every, None),)
        + (P(None, every),) * 5
        + (P(every, None), P(), P(), P(every, None), P(every, None))
    )
    return jax.shard_map(
        on_device, mesh=split, in_specs=placed, out_specs=P("tile", VIS, None), check_vma=False
    )
```

```python
import jax
import jax.numpy as jnp
from jax import lax
from jax.experimental import pallas as pl
from jax.experimental.pallas import tpu as pltpu
from jax.sharding import Mesh
from jax.sharding import PartitionSpec as P

ROWS = 1024
BLK = 8
SUB = 32
CHR = 16
POLC = 8
TAPS = 7
OS = 16
CAP = 4
N_VIS = 64
DATA = CHR * POLC
WIRE = BLK * DATA + 5 * BLK * CHR
PIECES = 128
FLAT = 4 * 256
WIDE = FLAT + 128
VIS = ("x", "zh", "zl", "core")
BF = jnp.bfloat16
F32 = jnp.float32
I32 = jnp.int32
VMEM_BYTES = 48 * 1024 * 1024


def pack_kernel(
    route_hbm, vis_hbm, uc_hbm, vc_hbm, uf_hbm, vf_hbm, w_hbm, out_ref, route_ref, vis_ref, code_ref, sems
):
    pairs = [(route_hbm, route_ref), (vis_hbm, vis_ref)]
    pairs += [
        (ref, code_ref.at[kind])
        for kind, ref in enumerate((uc_hbm, vc_hbm, uf_hbm, vf_hbm, w_hbm))
    ]
    copies = [
        pltpu.make_async_copy(source, target, sems.at[index])
        for index, (source, target) in enumerate(pairs)
    ]
    for copy in copies:
        copy.start()
    copies[0].wait()

    route = route_ref[...]
    route_f = route.astype(F32)
    column = jnp.transpose(jnp.broadcast_to(route_f, (8, ROWS)))[:, 0:1]
    parts = ROWS // 128
    before = lax.broadcasted_iota(I32, (128, 128), 0) < lax.broadcasted_iota(I32, (128, 128), 1)
    counts = [jnp.zeros((8, 128), F32) for _ in range(parts)]
    for first in range(parts):
        mine = jnp.broadcast_to(column[first * 128 : first * 128 + 128], (128, 128))
        for second in range(first, parts):
            same = mine == route_f[:, second * 128 : second * 128 + 128]
            if first == second:
                same = same & before
            same = jnp.where(same, 1.0, 0.0)
            counts[second] = counts[second] + jnp.sum(same.reshape(16, 8, 128), axis=0)
    rank = jnp.concatenate([jnp.sum(c, axis=0, keepdims=True) for c in counts], axis=1)
    rank_column = jnp.transpose(jnp.broadcast_to(rank, (8, ROWS)))[:, 0:1]
    block_row = lax.bitwise_and(route, BLK - 1)
    seat = lax.shift_right_logical(route, 3) * CAP + rank.astype(I32)
    block_column = lax.bitwise_and(column.astype(I32), BLK - 1).astype(F32)
    block_wide = jnp.broadcast_to(block_column, (ROWS, 128)).astype(BF)

    for copy in copies[1:]:
        copy.wait()
    vis = vis_ref[...]
    data = jnp.concatenate(
        [jnp.where(block_wide == jnp.asarray(b, BF), vis, jnp.zeros_like(vis)) for b in range(BLK)],
        axis=1,
    )
    codes = []
    for kind in range(5):
        values = code_ref[kind].astype(F32)
        codes += [jnp.where(block_row == b, values, 0.0) for b in range(BLK)]
    codes = jnp.concatenate(codes, axis=0).astype(BF)

    place = lax.broadcasted_iota(I32, (N_VIS * CAP, ROWS), 0)
    onehot = jnp.where(place == seat, 1.0, 0.0).astype(BF)
    left = jnp.dot(onehot, data, preferred_element_type=F32)
    out_ref[:, :, : BLK * DATA] = left.reshape(N_VIS, CAP, BLK * DATA).astype(BF)
    right = lax.dot_general(
        onehot, codes, (((1,), (1,)), ((), ())), preferred_element_type=F32
    )
    out_ref[:, :, BLK * DATA :] = right.reshape(N_VIS, CAP, 5 * BLK * CHR).astype(BF)


def grid_kernel(
    tile_ref, anchor_ref, recv_ref, taps_ref, taper_ref, out_ref, wide, indices, turned, codes, sums, rolled, send
):
    for part in range(WIRE // 128):
        wide[part] = recv_ref[:, part * 128 : part * 128 + 128].astype(F32)
    send[...] = jnp.zeros_like(send)
    taps = taps_ref[...]
    lane = lax.broadcasted_iota(I32, (8, 128), 1)
    sub8 = lax.broadcasted_iota(I32, (8, 128), 0)
    rows16 = lax.broadcasted_iota(I32, (16, 128), 0)
    low_lanes = lax.broadcasted_iota(I32, (SUB, 128), 1) < 64
    pair_of = [
        (2 * pair + jnp.where(rows16 < 8, 0, 1)).astype(F32).astype(BF) for pair in range(4)
    ]
    zero16 = jnp.zeros((16, 128), BF)

    def weights(cell_low, index):
        picked = jnp.take_along_axis(taps, jnp.broadcast_to(index, (8, 128)), axis=1)
        return jnp.take_along_axis(picked, (sub8 - cell_low) & 7, axis=0)

    def strip(part, r):
        return wide[part, pl.ds(r, N_VIS, stride=CAP), :]

    for kind in range(5):
        indices[kind] = jnp.transpose(
            jnp.concatenate([strip(BLK + kind, r) for r in range(CAP)], axis=0)
        )
    for block in range(BLK):
        turned[block] = jnp.transpose(
            jnp.concatenate([strip(block, r) for r in range(CAP)], axis=0)
        )
        at = block * CHR
        u_cell, v_cell, u_frac, v_frac, plane = [
            indices[kind, at : at + CHR, :].astype(I32) for kind in range(5)
        ]
        codes[block, 0] = u_cell & 7
        codes[block, 1] = lax.shift_right_logical(u_cell, 3)
        codes[block, 2] = v_cell & 7
        codes[block, 3] = lax.shift_right_logical(v_cell, 3)
        codes[block, 4] = plane * OS + u_frac
        codes[block, 5] = plane * OS + v_frac

    def one_block(block, carry):
        total = jnp.zeros((128, 128), F32)
        for h in range(CHR):
            a_halves, b_halves = [], []
            for half in range(2):
                at = slice(half * 128, half * 128 + 128)
                u_low, u_high, v_low, v_high, u_index, v_index = [
                    jnp.broadcast_to(codes[block, kind, h : h + 1, at], (8, 128))
                    for kind in range(6)
                ]
                turn_u = weights(u_low, u_index)
                turn_v = weights(v_low, v_index)
                samples = turned[block, h * POLC : (h + 1) * POLC, at]
                group_v = v_high + jnp.where(sub8 < v_low, 1, 0)
                weight_v = [jnp.where(group_v == g, turn_v, 0.0) for g in range(4)]
                weight_v = [
                    jnp.concatenate(weight_v[2 * g : 2 * g + 2], axis=0).astype(BF)
                    for g in range(2)
                ]
                high = u_high.astype(F32)
                high = jnp.concatenate([high, high], axis=0).astype(BF)
                b_rows = []
                for g in range(4):
                    mask = high == jnp.asarray(g, BF)
                    b_rows += [jnp.where(mask, part, zero16) for part in weight_v]
                b_halves.append(jnp.concatenate(b_rows, axis=0))
                low = u_low.astype(F32)
                low = jnp.concatenate([low, low], axis=0).astype(BF)
                same, later = [], []
                for pair in range(4):
                    product = [
                        jnp.broadcast_to(turn_u[s : s + 1], (8, 128)) * samples
                        for s in (2 * pair, 2 * pair + 1)
                    ]
                    product = jnp.concatenate(product, axis=0).astype(BF)
                    mask = low <= pair_of[pair]
                    same.append(jnp.where(mask, product, zero16))
                    later.append(jnp.where(mask, zero16, product))
                a_halves.append(jnp.concatenate(same + later, axis=0))
            total = total + lax.dot_general(
                jnp.concatenate(b_halves, axis=1),
                jnp.concatenate(a_halves, axis=1),
                (((1,), (1,)), ((), ())),
                preferred_element_type=F32,
            )
        sums[block] = total
        return carry

    lax.fori_loop(0, BLK, one_block, 0, unroll=8)

    taper = taper_ref[...]
    tiles = [tile_ref[block, 0] for block in range(BLK)]
    groups = [lax.div(tile, 2) for tile in tiles]
    for block in range(BLK):
        total = sums[block]
        crossed = pltpu.roll(total, 64, 1)
        anchor_v, anchor_u = anchor_ref[block, 0], anchor_ref[block, 1]
        shift_v = lax.rem(anchor_v, SUB)
        shift_u = lax.rem(anchor_u, SUB) * POLC
        sides = []
        for side in range(2):
            before = crossed[32:64] if side else jnp.zeros((SUB, 128), F32)
            after = crossed[96:128] if side else crossed[32:64]
            sides.append(total[side * 64 : side * 64 + 32] + jnp.where(low_lanes, before, after))
        grid = jnp.concatenate(sides, axis=1) * taper
        grid = pltpu.roll(grid, shift_v, 0)
        grid = pltpu.roll(grid, shift_u, 1)
        for side in range(2):
            rolled[block, side] = grid[:, side * 128 : side * 128 + 128]
        order = jnp.int32(0)
        for other in range(block):
            order = order + jnp.where(groups[other] == groups[block], 1, 0)
        row = groups[block] * CAP + order
        for k in range(4):
            for side in range(2):
                send[k * 2 + side, pl.ds(row, 8, stride=16), :] = rolled[
                    block, side, pl.ds(k, 8, stride=4), :
                ]
        meta = jnp.where(lane == 0, 1 + lax.rem(tiles[block], 2), 0)
        meta = jnp.where(lane == 1, lax.div(anchor_v, SUB), meta)
        meta = jnp.where(lane == 2, shift_v - 4 * sub8, meta)
        meta = jnp.where(lane == 3, lax.div(anchor_u, SUB), meta)
        meta = jnp.where(lane == 4, shift_u, meta)
        send[8, pl.ds(row, 8, stride=16), :] = meta.astype(F32)
    for part in range(WIDE // 128):
        out_ref[:, part * 128 : part * 128 + 128] = send[part].astype(BF)


def place_kernel(recv_ref, out_ref):
    meta = recv_ref[:, FLAT:WIDE].astype(F32)
    kind, row_y, edge_v, row_x, edge_u = [
        meta[:, k : k + 1].astype(I32) for k in range(5)
    ]
    data = recv_ref[:, :FLAT].astype(F32)
    spot = lax.broadcasted_iota(I32, (PIECES, FLAT), 1)
    late_v = lax.shift_right_logical(spot, 8) < edge_v
    late_u = lax.bitwise_and(spot, 255) < edge_u
    target = lax.broadcasted_iota(I32, (PIECES, PIECES), 1)
    first = jnp.where(kind > 0, row_y * 16 + (kind - 1) * 8 + row_x, -64)
    picks, pieces = [], []
    for down in range(2):
        for right in range(2):
            keep_v = late_v if down else jnp.logical_not(late_v)
            keep_u = late_u if right else jnp.logical_not(late_u)
            pieces.append(jnp.where(keep_v & keep_u, data, 0.0).astype(BF))
            picks.append(
                jnp.where(target == first + (16 * down + right), 1.0, 0.0)
            )
    pick = jnp.concatenate(picks, axis=0)
    piece = jnp.concatenate(pieces, axis=0)
    pick = jnp.transpose(pick).astype(BF)
    out_ref[...] = jnp.dot(pick, piece, preferred_element_type=F32).astype(BF)


def total_kernel(recv_ref, out_ref):
    total = recv_ref[0:16, :].astype(F32)
    for source in range(1, 8):
        total = total + recv_ref[source * 16 : source * 16 + 16, :].astype(F32)
    for tile in range(2):
        for across in range(8):
            for k in range(4):
                row = tile * 8 + across
                out_ref[tile, k : k + 1, across * 256 : across * 256 + 256] = total[
                    row : row + 1, k * 256 : k * 256 + 256
                ]


PACK_BYTES = None
PACK_SCRATCH = [
    pltpu.VMEM((1, ROWS), I32),
    pltpu.VMEM((ROWS, DATA), BF),
    pltpu.VMEM((5, CHR, ROWS), I32),
    pltpu.SemaphoreType.DMA((7,)),
]
GRID_SCRATCH = [
    pltpu.VMEM((WIRE // 128, N_VIS * CAP, 128), F32),
    pltpu.VMEM((5, BLK * CHR, N_VIS * CAP), F32),
    pltpu.VMEM((BLK, DATA, N_VIS * CAP), F32),
    pltpu.VMEM((BLK, 6, CHR, N_VIS * CAP), I32),
    pltpu.VMEM((BLK, 128, 128), F32),
    pltpu.VMEM((BLK, 2, SUB, 128), F32),
    pltpu.VMEM((WIDE // 128, PIECES, 128), F32),
]


def call(
    kernel, shape, dtype, spaces, scratch=(), flops=0, moved=0, out=pltpu.VMEM, limit=VMEM_BYTES
):
    specs = [pl.BlockSpec(memory_space=space) for space in spaces]
    return pl.pallas_call(
        kernel,
        out_shape=jax.ShapeDtypeStruct(shape, dtype),
        in_specs=specs,
        out_specs=pl.BlockSpec(memory_space=out),
        scratch_shapes=list(scratch),
        compiler_params=pltpu.CompilerParams(vmem_limit_bytes=limit),
        cost_estimate=pl.CostEstimate(flops=flops, bytes_accessed=moved, transcendentals=0),
    )


def on_device(
    vis_data,
    u_cell,
    v_cell,
    u_frac,
    v_frac,
    w_plane,
    block_route,
    kernel_taps,
    taper_gain,
    sub_tile,
    sub_anchor,
):
    vm, sm, hbm = pltpu.VMEM, pltpu.SMEM, pltpu.HBM
    packed = call(
        pack_kernel,
        (N_VIS, CAP, WIRE),
        BF,
        [hbm] * 7,
        scratch=PACK_SCRATCH,
        flops=1 << 30,
        moved=2 << 20,
        limit=PACK_BYTES,
    )(block_route.reshape(1, ROWS), vis_data, u_cell, v_cell, u_frac, v_frac, w_plane)
    rows = lax.all_to_all(
        packed, VIS, split_axis=0, concat_axis=0, tiled=True
    ).reshape(N_VIS * CAP, WIRE)

    taps = jnp.zeros((8, 128), F32).at[:TAPS].set(kernel_taps.T.astype(BF).astype(F32))
    taper = jnp.repeat(taper_gain, POLC, axis=1)
    pieces = call(
        grid_kernel,
        (PIECES, WIDE),
        BF,
        [sm, sm, vm, vm, vm],
        scratch=GRID_SCRATCH,
        flops=1 << 32,
        moved=2 << 20,
    )(sub_tile, sub_anchor, rows, taps, taper)
    pieces = lax.all_to_all(
        pieces.reshape(32, CAP, WIDE),
        ("zl", "core", "tile"),
        split_axis=0,
        concat_axis=0,
        tiled=True,
    ).reshape(PIECES, WIDE)
    canvas = call(place_kernel, (PIECES, FLAT), BF, [vm], flops=1 << 27, moved=1 << 19)(pieces)
    canvas = lax.all_to_all(
        canvas.reshape(8, 16, FLAT), ("x", "zh"), split_axis=0, concat_axis=0, tiled=True
    ).reshape(PIECES, FLAT)
    return call(total_kernel, (2, 4, 2048), F32, [vm], moved=1 << 19)(canvas)


def solution(mesh):
    split = Mesh(
        mesh.devices.reshape(4, 2, 4, 2, 4), ("x", "zh", "zl", "core", "tile")
    )
    every = VIS + ("tile",)
    placed = (
        (P(every, None),)
        + (P(None, every),) * 5
        + (P(every, None), P(), P(), P(every, None), P(every, None))
    )
    return jax.shard_map(
        on_device, mesh=split, in_specs=placed, out_specs=P("tile", VIS, None), check_vma=False
    )
```

```python
import jax
import jax.numpy as jnp
from jax import lax
from jax.experimental import pallas as pl
from jax.experimental.pallas import tpu as pltpu
from jax.sharding import Mesh
from jax.sharding import PartitionSpec as P

ROWS = 1024
BLK = 8
SUB = 32
CHR = 16
POLC = 8
TAPS = 7
OS = 16
CAP = 4
N_VIS = 64
DATA = CHR * POLC
WIRE = BLK * DATA + 5 * BLK * CHR
PIECES = 128
FLAT = 4 * 256
WIDE = FLAT + 128
VIS = ("x", "zh", "zl", "core")
BF = jnp.bfloat16
F32 = jnp.float32
I32 = jnp.int32
VMEM_BYTES = 48 * 1024 * 1024


def pack_kernel(
    route_hbm, vis_hbm, uc_hbm, vc_hbm, uf_hbm, vf_hbm, w_hbm, out_hbm, route_ref, vis_ref, code_ref, line_ref, sems
):
    pairs = [(route_hbm, route_ref), (vis_hbm, vis_ref)]
    pairs += [
        (ref, code_ref.at[kind])
        for kind, ref in enumerate((uc_hbm, vc_hbm, uf_hbm, vf_hbm, w_hbm))
    ]
    copies = [
        pltpu.make_async_copy(source, target, sems.at[index])
        for index, (source, target) in enumerate(pairs)
    ]
    for copy in copies:
        copy.start()
    copies[0].wait()

    route = route_ref[...]
    route_f = route.astype(F32)
    column = jnp.transpose(jnp.broadcast_to(route_f, (8, ROWS)))[:, 0:1]
    parts = ROWS // 128
    before = lax.broadcasted_iota(I32, (128, 128), 0) < lax.broadcasted_iota(I32, (128, 128), 1)
    counts = [jnp.zeros((8, 128), F32) for _ in range(parts)]
    for first in range(parts):
        mine = jnp.broadcast_to(column[first * 128 : first * 128 + 128], (128, 128))
        for second in range(first, parts):
            same = mine == route_f[:, second * 128 : second * 128 + 128]
            if first == second:
                same = same & before
            same = jnp.where(same, 1.0, 0.0)
            counts[second] = counts[second] + jnp.sum(same.reshape(16, 8, 128), axis=0)
    rank = jnp.concatenate([jnp.sum(c, axis=0, keepdims=True) for c in counts], axis=1)
    rank_column = jnp.transpose(jnp.broadcast_to(rank, (8, ROWS)))[:, 0:1]
    block_row = lax.bitwise_and(route, BLK - 1)
    seat = lax.shift_right_logical(route, 3) * CAP + rank.astype(I32)
    block_column = lax.bitwise_and(column.astype(I32), BLK - 1).astype(F32)
    block_wide = jnp.broadcast_to(block_column, (ROWS, 128)).astype(BF)

    for copy in copies[1:]:
        copy.wait()
    vis = vis_ref[...]
    data = jnp.concatenate(
        [jnp.where(block_wide == jnp.asarray(b, BF), vis, jnp.zeros_like(vis)) for b in range(BLK)],
        axis=1,
    )
    codes = []
    for kind in range(5):
        values = code_ref[kind].astype(F32)
        codes += [jnp.where(block_row == b, values, 0.0) for b in range(BLK)]
    codes = jnp.concatenate(codes, axis=0).astype(BF)

    place = lax.broadcasted_iota(I32, (N_VIS * CAP, ROWS), 0)
    onehot = jnp.where(place == seat, 1.0, 0.0).astype(BF)
    leaving = []

    def leave(first, last):
        columns = pl.ds(first, last - first)
        leaving.append(
            pltpu.make_async_copy(
                line_ref.at[:, :, columns], out_hbm.at[:, :, columns], sems.at[7 + len(leaving)]
            )
        )
        leaving[-1].start()

    right = lax.dot_general(
        onehot, codes, (((1,), (1,)), ((), ())), preferred_element_type=F32
    )
    line_ref[:, :, BLK * DATA :] = right.reshape(N_VIS, CAP, 5 * BLK * CHR).astype(BF)
    leave(BLK * DATA, WIRE)
    part = 512
    for first in range(0, BLK * DATA, part):
        left = jnp.dot(onehot, data[:, first : first + part], preferred_element_type=F32)
        line_ref[:, :, first : first + part] = left.reshape(N_VIS, CAP, part).astype(BF)
        leave(first, first + part)
    for copy in leaving:
        copy.wait()


def grid_kernel(
    tile_ref, anchor_ref, recv_ref, taps_ref, taper_ref, out_ref, wide, indices, turned, codes, sums, rolled, send
):
    for part in range(WIRE // 128):
        wide[part] = recv_ref[:, part * 128 : part * 128 + 128].astype(F32)
    send[...] = jnp.zeros_like(send)
    taps = taps_ref[...]
    lane = lax.broadcasted_iota(I32, (8, 128), 1)
    sub8 = lax.broadcasted_iota(I32, (8, 128), 0)
    rows16 = lax.broadcasted_iota(I32, (16, 128), 0)
    low_lanes = lax.broadcasted_iota(I32, (SUB, 128), 1) < 64
    pair_of = [
        (2 * pair + jnp.where(rows16 < 8, 0, 1)).astype(F32).astype(BF) for pair in range(4)
    ]
    zero16 = jnp.zeros((16, 128), BF)

    def weights(cell_low, index):
        picked = jnp.take_along_axis(taps, jnp.broadcast_to(index, (8, 128)), axis=1)
        return jnp.take_along_axis(picked, (sub8 - cell_low) & 7, axis=0)

    def strip(part, r):
        return wide[part, pl.ds(r, N_VIS, stride=CAP), :]

    for kind in range(5):
        indices[kind] = jnp.transpose(
            jnp.concatenate([strip(BLK + kind, r) for r in range(CAP)], axis=0)
        )
    for block in range(BLK):
        turned[block] = jnp.transpose(
            jnp.concatenate([strip(block, r) for r in range(CAP)], axis=0)
        )
        at = block * CHR
        u_cell, v_cell, u_frac, v_frac, plane = [
            indices[kind, at : at + CHR, :].astype(I32) for kind in range(5)
        ]
        codes[block, 0] = u_cell & 7
        codes[block, 1] = lax.shift_right_logical(u_cell, 3)
        codes[block, 2] = v_cell & 7
        codes[block, 3] = lax.shift_right_logical(v_cell, 3)
        codes[block, 4] = plane * OS + u_frac
        codes[block, 5] = plane * OS + v_frac

    def one_block(block, carry):
        total = jnp.zeros((128, 128), F32)
        for h in range(CHR):
            a_halves, b_halves = [], []
            for half in range(2):
                at = slice(half * 128, half * 128 + 128)
                u_low, u_high, v_low, v_high, u_index, v_index = [
                    jnp.broadcast_to(codes[block, kind, h : h + 1, at], (8, 128))
                    for kind in range(6)
                ]
                turn_u = weights(u_low, u_index)
                turn_v = weights(v_low, v_index)
                samples = turned[block, h * POLC : (h + 1) * POLC, at]
                group_v = v_high + jnp.where(sub8 < v_low, 1, 0)
                weight_v = [jnp.where(group_v == g, turn_v, 0.0) for g in range(4)]
                weight_v = [
                    jnp.concatenate(weight_v[2 * g : 2 * g + 2], axis=0).astype(BF)
                    for g in range(2)
                ]
                high = u_high.astype(F32)
                high = jnp.concatenate([high, high], axis=0).astype(BF)
                b_rows = []
                for g in range(4):
                    mask = high == jnp.asarray(g, BF)
                    b_rows += [jnp.where(mask, part, zero16) for part in weight_v]
                b_halves.append(jnp.concatenate(b_rows, axis=0))
                low = u_low.astype(F32)
                low = jnp.concatenate([low, low], axis=0).astype(BF)
                same, later = [], []
                for pair in range(4):
                    product = [
                        jnp.broadcast_to(turn_u[s : s + 1], (8, 128)) * samples
                        for s in (2 * pair, 2 * pair + 1)
                    ]
                    product = jnp.concatenate(product, axis=0).astype(BF)
                    mask = low <= pair_of[pair]
                    same.append(jnp.where(mask, product, zero16))
                    later.append(jnp.where(mask, zero16, product))
                a_halves.append(jnp.concatenate(same + later, axis=0))
            total = total + lax.dot_general(
                jnp.concatenate(a_halves, axis=1),
                jnp.concatenate(b_halves, axis=1),
                (((1,), (1,)), ((), ())),
                preferred_element_type=F32,
            )
        sums[block] = jnp.transpose(total)
        return carry

    lax.fori_loop(0, BLK, one_block, 0, unroll=8)

    taper = taper_ref[...]
    tiles = [tile_ref[block, 0] for block in range(BLK)]
    groups = [lax.div(tile, 2) for tile in tiles]
    for block in range(BLK):
        total = sums[block]
        crossed = pltpu.roll(total, 64, 1)
        anchor_v, anchor_u = anchor_ref[block, 0], anchor_ref[block, 1]
        shift_v = lax.rem(anchor_v, SUB)
        shift_u = lax.rem(anchor_u, SUB) * POLC
        sides = []
        for side in range(2):
            before = crossed[32:64] if side else jnp.zeros((SUB, 128), F32)
            after = crossed[96:128] if side else crossed[32:64]
            sides.append(total[side * 64 : side * 64 + 32] + jnp.where(low_lanes, before, after))
        grid = jnp.concatenate(sides, axis=1) * taper
        grid = pltpu.roll(grid, shift_v, 0)
        grid = pltpu.roll(grid, shift_u, 1)
        for side in range(2):
            rolled[block, side] = grid[:, side * 128 : side * 128 + 128]
        order = jnp.int32(0)
        for other in range(block):
            order = order + jnp.where(groups[other] == groups[block], 1, 0)
        row = groups[block] * CAP + order
        for k in range(4):
            for side in range(2):
                send[k * 2 + side, pl.ds(row, 8, stride=16), :] = rolled[
                    block, side, pl.ds(k, 8, stride=4), :
                ]
        meta = jnp.where(lane == 0, 1 + lax.rem(tiles[block], 2), 0)
        meta = jnp.where(lane == 1, lax.div(anchor_v, SUB), meta)
        meta = jnp.where(lane == 2, shift_v - 4 * sub8, meta)
        meta = jnp.where(lane == 3, lax.div(anchor_u, SUB), meta)
        meta = jnp.where(lane == 4, shift_u, meta)
        send[8, pl.ds(row, 8, stride=16), :] = meta.astype(F32)
    for part in range(WIDE // 128):
        lanes = send[part].reshape(PIECES // CAP, CAP, 128)
        out_ref[:, :, part * 128 : part * 128 + 128] = lanes.astype(BF)


def place_kernel(recv_ref, out_ref):
    meta = recv_ref[:, FLAT:WIDE].astype(F32)
    kind, row_y, edge_v, row_x, edge_u = [
        meta[:, k : k + 1].astype(I32) for k in range(5)
    ]
    data = recv_ref[:, :FLAT].astype(F32)
    spot = lax.broadcasted_iota(I32, (PIECES, FLAT), 1)
    late_v = lax.shift_right_logical(spot, 8) < edge_v
    late_u = lax.bitwise_and(spot, 255) < edge_u
    target = lax.broadcasted_iota(I32, (PIECES, PIECES), 1)
    first = jnp.where(kind > 0, row_y * 16 + (kind - 1) * 8 + row_x, -64)
    picks, pieces = [], []
    for down in range(2):
        for right in range(2):
            keep_v = late_v if down else jnp.logical_not(late_v)
            keep_u = late_u if right else jnp.logical_not(late_u)
            pieces.append(jnp.where(keep_v & keep_u, data, 0.0).astype(BF))
            picks.append(
                jnp.where(target == first + (16 * down + right), 1.0, 0.0)
            )
    pick = jnp.concatenate(picks, axis=0)
    piece = jnp.concatenate(pieces, axis=0)
    pick = jnp.transpose(pick).astype(BF)
    out_ref[...] = jnp.dot(pick, piece, preferred_element_type=F32).astype(BF)


def total_kernel(recv_ref, out_ref):
    total = recv_ref[0:16, :].astype(F32)
    for source in range(1, 8):
        total = total + recv_ref[source * 16 : source * 16 + 16, :].astype(F32)
    for tile in range(2):
        for across in range(8):
            for k in range(4):
                row = tile * 8 + across
                out_ref[tile, k : k + 1, across * 256 : across * 256 + 256] = total[
                    row : row + 1, k * 256 : k * 256 + 256
                ]


PACK_BYTES = None
PACK_SCRATCH = [
    pltpu.VMEM((1, ROWS), I32),
    pltpu.VMEM((ROWS, DATA), BF),
    pltpu.VMEM((5, CHR, ROWS), I32),
    pltpu.VMEM((N_VIS, CAP, WIRE), BF),
    pltpu.SemaphoreType.DMA((10,)),
]
GRID_SCRATCH = [
    pltpu.VMEM((WIRE // 128, N_VIS * CAP, 128), F32),
    pltpu.VMEM((5, BLK * CHR, N_VIS * CAP), F32),
    pltpu.VMEM((BLK, DATA, N_VIS * CAP), F32),
    pltpu.VMEM((BLK, 6, CHR, N_VIS * CAP), I32),
    pltpu.VMEM((BLK, 128, 128), F32),
    pltpu.VMEM((BLK, 2, SUB, 128), F32),
    pltpu.VMEM((WIDE // 128, PIECES, 128), F32),
]


def call(
    kernel, shape, dtype, spaces, scratch=(), flops=0, moved=0, out=pltpu.VMEM, limit=VMEM_BYTES
):
    specs = [pl.BlockSpec(memory_space=space) for space in spaces]
    return pl.pallas_call(
        kernel,
        out_shape=jax.ShapeDtypeStruct(shape, dtype),
        in_specs=specs,
        out_specs=pl.BlockSpec(memory_space=out),
        scratch_shapes=list(scratch),
        compiler_params=pltpu.CompilerParams(vmem_limit_bytes=limit),
        cost_estimate=pl.CostEstimate(flops=flops, bytes_accessed=moved, transcendentals=0),
    )


def on_device(
    vis_data,
    u_cell,
    v_cell,
    u_frac,
    v_frac,
    w_plane,
    block_route,
    kernel_taps,
    taper_gain,
    sub_tile,
    sub_anchor,
):
    vm, sm, hbm = pltpu.VMEM, pltpu.SMEM, pltpu.HBM
    packed = call(
        pack_kernel,
        (N_VIS, CAP, WIRE),
        BF,
        [hbm] * 7,
        scratch=PACK_SCRATCH,
        flops=1 << 30,
        moved=2 << 20,
        out=hbm,
        limit=PACK_BYTES,
    )(block_route.reshape(1, ROWS), vis_data, u_cell, v_cell, u_frac, v_frac, w_plane)
    rows = lax.all_to_all(
        packed, VIS, split_axis=0, concat_axis=0, tiled=True
    ).reshape(N_VIS * CAP, WIRE)

    taps = jnp.zeros((8, 128), F32).at[:TAPS].set(kernel_taps.T.astype(BF).astype(F32))
    taper = jnp.repeat(taper_gain, POLC, axis=1)
    pieces = call(
        grid_kernel,
        (PIECES // CAP, CAP, WIDE),
        BF,
        [sm, sm, vm, vm, vm],
        scratch=GRID_SCRATCH,
        flops=1 << 32,
        moved=2 << 20,
    )(sub_tile, sub_anchor, rows, taps, taper)
    pieces = lax.all_to_all(
        pieces,
        ("zl", "core", "tile"),
        split_axis=0,
        concat_axis=0,
        tiled=True,
    ).reshape(PIECES, WIDE)
    canvas = call(place_kernel, (PIECES, FLAT), BF, [vm], flops=1 << 27, moved=1 << 19)(pieces)
    canvas = lax.all_to_all(
        canvas.reshape(8, 16, FLAT), ("x", "zh"), split_axis=0, concat_axis=0, tiled=True
    ).reshape(PIECES, FLAT)
    return call(total_kernel, (2, 4, 2048), F32, [vm], moved=1 << 19)(canvas)


def solution(mesh):
    split = Mesh(
        mesh.devices.reshape(4, 2, 4, 2, 4), ("x", "zh", "zl", "core", "tile")
    )
    every = VIS + ("tile",)
    placed = (
        (P(every, None),)
        + (P(None, every),) * 5
        + (P(every, None), P(), P(), P(every, None), P(every, None))
    )
    return jax.shard_map(
        on_device, mesh=split, in_specs=placed, out_specs=P("tile", VIS, None), check_vma=False
    )
```

```python
import jax
import jax.numpy as jnp
from jax import lax
from jax.experimental import pallas as pl
from jax.experimental.pallas import tpu as pltpu
from jax.sharding import Mesh
from jax.sharding import PartitionSpec as P

ROWS = 1024
BLK = 8
SUB = 32
CHR = 16
POLC = 8
TAPS = 7
OS = 16
CAP = 4
N_VIS = 64
DATA = CHR * POLC
WIRE = BLK * DATA + 5 * BLK * CHR
PIECES = 128
FLAT = 4 * 256
WIDE = FLAT + 128
VIS = ("x", "zh", "zl", "core")
BF = jnp.bfloat16
F32 = jnp.float32
I32 = jnp.int32
VMEM_BYTES = 48 * 1024 * 1024


def pack_kernel(
    route_hbm, vis_hbm, uc_hbm, vc_hbm, uf_hbm, vf_hbm, w_hbm, out_hbm, route_ref, vis_ref, code_ref, line_ref, sems
):
    pairs = [(route_hbm, route_ref), (vis_hbm, vis_ref)]
    pairs += [
        (ref, code_ref.at[kind])
        for kind, ref in enumerate((uc_hbm, vc_hbm, uf_hbm, vf_hbm, w_hbm))
    ]
    copies = [
        pltpu.make_async_copy(source, target, sems.at[index])
        for index, (source, target) in enumerate(pairs)
    ]
    for copy in copies:
        copy.start()
    copies[0].wait()

    route = route_ref[...]
    route_f = route.astype(F32)
    column = jnp.transpose(jnp.broadcast_to(route_f, (8, ROWS)))[:, 0:1]
    parts = ROWS // 128
    before = lax.broadcasted_iota(I32, (128, 128), 0) < lax.broadcasted_iota(I32, (128, 128), 1)
    counts = [jnp.zeros((8, 128), F32) for _ in range(parts)]
    for first in range(parts):
        mine = jnp.broadcast_to(column[first * 128 : first * 128 + 128], (128, 128))
        for second in range(first, parts):
            same = mine == route_f[:, second * 128 : second * 128 + 128]
            if first == second:
                same = same & before
            same = jnp.where(same, 1.0, 0.0)
            counts[second] = counts[second] + jnp.sum(same.reshape(16, 8, 128), axis=0)
    rank = jnp.concatenate([jnp.sum(c, axis=0, keepdims=True) for c in counts], axis=1)
    rank_column = jnp.transpose(jnp.broadcast_to(rank, (8, ROWS)))[:, 0:1]
    block_row = lax.bitwise_and(route, BLK - 1)
    seat = lax.shift_right_logical(route, 3) * CAP + rank.astype(I32)
    block_column = lax.bitwise_and(column.astype(I32), BLK - 1).astype(F32)
    block_wide = jnp.broadcast_to(block_column, (ROWS, 128)).astype(BF)

    for copy in copies[1:]:
        copy.wait()
    vis = vis_ref[...]
    data = jnp.concatenate(
        [jnp.where(block_wide == jnp.asarray(b, BF), vis, jnp.zeros_like(vis)) for b in range(BLK)],
        axis=1,
    )
    codes = []
    for kind in range(5):
        values = code_ref[kind].astype(F32)
        codes += [jnp.where(block_row == b, values, 0.0) for b in range(BLK)]
    codes = jnp.concatenate(codes, axis=0).astype(BF)

    place = lax.broadcasted_iota(I32, (N_VIS * CAP, ROWS), 0)
    onehot = jnp.where(place == seat, 1.0, 0.0).astype(BF)
    leaving = []

    def leave(first, last):
        columns = pl.ds(first, last - first)
        leaving.append(
            pltpu.make_async_copy(
                line_ref.at[:, :, columns], out_hbm.at[:, :, columns], sems.at[7 + len(leaving)]
            )
        )
        leaving[-1].start()

    right = lax.dot_general(
        onehot, codes, (((1,), (1,)), ((), ())), preferred_element_type=F32
    )
    line_ref[:, :, BLK * DATA :] = right.reshape(N_VIS, CAP, 5 * BLK * CHR).astype(BF)
    leave(BLK * DATA, WIRE)
    part = 512
    for first in range(0, BLK * DATA, part):
        left = jnp.dot(onehot, data[:, first : first + part], preferred_element_type=F32)
        line_ref[:, :, first : first + part] = left.reshape(N_VIS, CAP, part).astype(BF)
        leave(first, first + part)
    for copy in leaving:
        copy.wait()


def grid_kernel(
    tile_ref, anchor_ref, recv_ref, taps_ref, taper_ref, out_ref, wide, indices, turned, codes, sums, rolled, send
):
    for part in range(WIRE // 128):
        wide[part, : N_VIS * CAP] = recv_ref[:, part * 128 : part * 128 + 128].astype(F32)
    send[...] = jnp.zeros_like(send)
    taps = taps_ref[...]
    lane = lax.broadcasted_iota(I32, (8, 128), 1)
    sub8 = lax.broadcasted_iota(I32, (8, 128), 0)
    rows16 = lax.broadcasted_iota(I32, (16, 128), 0)
    low_lanes = lax.broadcasted_iota(I32, (SUB, 128), 1) < 64
    pair_of = [
        (2 * pair + jnp.where(rows16 < 8, 0, 1)).astype(F32).astype(BF) for pair in range(4)
    ]
    zero16 = jnp.zeros((16, 128), BF)

    def weights(cell_low, index):
        picked = jnp.take_along_axis(taps, jnp.broadcast_to(index, (8, 128)), axis=1)
        return jnp.take_along_axis(picked, (sub8 - cell_low) & 7, axis=0)

    def strip(part, r):
        return wide[part, pl.ds(r, N_VIS, stride=CAP), :]

    for kind in range(5):
        indices[kind] = jnp.transpose(
            jnp.concatenate([strip(BLK + kind, r) for r in range(CAP)], axis=0)
        )
    for block in range(BLK):
        turned[block] = jnp.transpose(
            jnp.concatenate([strip(block, r) for r in range(CAP)], axis=0)
        )
        at = block * CHR
        u_cell, v_cell, u_frac, v_frac, plane = [
            indices[kind, at : at + CHR, :].astype(I32) for kind in range(5)
        ]
        codes[block, 0] = u_cell & 7
        codes[block, 1] = lax.shift_right_logical(u_cell, 3)
        codes[block, 2] = v_cell & 7
        codes[block, 3] = lax.shift_right_logical(v_cell, 3)
        codes[block, 4] = plane * OS + u_frac
        codes[block, 5] = plane * OS + v_frac

    def one_block(block, carry):
        total = jnp.zeros((128, 128), F32)
        for h in range(CHR):
            a_halves, b_halves = [], []
            for half in range(2):
                at = slice(half * 128, half * 128 + 128)
                u_low, u_high, v_low, v_high, u_index, v_index = [
                    jnp.broadcast_to(codes[block, kind, h : h + 1, at], (8, 128))
                    for kind in range(6)
                ]
                turn_u = weights(u_low, u_index)
                turn_v = weights(v_low, v_index)
                samples = turned[block, h * POLC : (h + 1) * POLC, at]
                group_v = v_high + jnp.where(sub8 < v_low, 1, 0)
                weight_v = [jnp.where(group_v == g, turn_v, 0.0) for g in range(4)]
                weight_v = [
                    jnp.concatenate(weight_v[2 * g : 2 * g + 2], axis=0).astype(BF)
                    for g in range(2)
                ]
                high = u_high.astype(F32)
                high = jnp.concatenate([high, high], axis=0).astype(BF)
                b_rows = []
                for g in range(4):
                    mask = high == jnp.asarray(g, BF)
                    b_rows += [jnp.where(mask, part, zero16) for part in weight_v]
                b_halves.append(jnp.concatenate(b_rows, axis=0))
                low = u_low.astype(F32)
                low = jnp.concatenate([low, low], axis=0).astype(BF)
                same, later = [], []
                for pair in range(4):
                    product = [
                        jnp.broadcast_to(turn_u[s : s + 1], (8, 128)) * samples
                        for s in (2 * pair, 2 * pair + 1)
                    ]
                    product = jnp.concatenate(product, axis=0).astype(BF)
                    mask = low <= pair_of[pair]
                    same.append(jnp.where(mask, product, zero16))
                    later.append(jnp.where(mask, zero16, product))
                a_halves.append(jnp.concatenate(same + later, axis=0))
            total = total + lax.dot_general(
                jnp.concatenate(a_halves, axis=1),
                jnp.concatenate(b_halves, axis=1),
                (((1,), (1,)), ((), ())),
                preferred_element_type=F32,
            )
        sums[block] = jnp.transpose(total)
        return carry

    lax.fori_loop(0, BLK, one_block, 0, unroll=8)

    taper = taper_ref[...]
    tiles = [tile_ref[block, 0] for block in range(BLK)]
    groups = [lax.div(tile, 2) for tile in tiles]
    for block in range(BLK):
        total = sums[block]
        crossed = pltpu.roll(total, 64, 1)
        anchor_v, anchor_u = anchor_ref[block, 0], anchor_ref[block, 1]
        shift_v = lax.rem(anchor_v, SUB)
        shift_u = lax.rem(anchor_u, SUB) * POLC
        sides = []
        for side in range(2):
            before = crossed[32:64] if side else jnp.zeros((SUB, 128), F32)
            after = crossed[96:128] if side else crossed[32:64]
            sides.append(total[side * 64 : side * 64 + 32] + jnp.where(low_lanes, before, after))
        grid = jnp.concatenate(sides, axis=1) * taper
        grid = pltpu.roll(grid, shift_v, 0)
        grid = pltpu.roll(grid, shift_u, 1)
        for side in range(2):
            rolled[block, side, :SUB] = grid[:, side * 128 : side * 128 + 128]
        order = jnp.int32(0)
        for other in range(block):
            order = order + jnp.where(groups[other] == groups[block], 1, 0)
        row = groups[block] * CAP + order
        for k in range(4):
            for side in range(2):
                send[k * 2 + side, pl.ds(row, 8, stride=16), :] = rolled[
                    block, side, pl.ds(k, 8, stride=4), :
                ]
        meta = jnp.where(lane == 0, 1 + lax.rem(tiles[block], 2), 0)
        meta = jnp.where(lane == 1, lax.div(anchor_v, SUB), meta)
        meta = jnp.where(lane == 2, shift_v - 4 * sub8, meta)
        meta = jnp.where(lane == 3, lax.div(anchor_u, SUB), meta)
        meta = jnp.where(lane == 4, shift_u, meta)
        send[8, pl.ds(row, 8, stride=16), :] = meta.astype(F32)
    for part in range(WIDE // 128):
        lanes = send[part, :PIECES].reshape(PIECES // CAP, CAP, 128)
        out_ref[:, :, part * 128 : part * 128 + 128] = lanes.astype(BF)


def place_kernel(recv_ref, out_ref):
    meta = recv_ref[:, FLAT:WIDE].astype(F32)
    kind, row_y, edge_v, row_x, edge_u = [
        meta[:, k : k + 1].astype(I32) for k in range(5)
    ]
    data = recv_ref[:, :FLAT].astype(F32)
    spot = lax.broadcasted_iota(I32, (PIECES, FLAT), 1)
    late_v = lax.shift_right_logical(spot, 8) < edge_v
    late_u = lax.bitwise_and(spot, 255) < edge_u
    target = lax.broadcasted_iota(I32, (PIECES, PIECES), 1)
    first = jnp.where(kind > 0, row_y * 16 + (kind - 1) * 8 + row_x, -64)
    picks, pieces = [], []
    for down in range(2):
        for right in range(2):
            keep_v = late_v if down else jnp.logical_not(late_v)
            keep_u = late_u if right else jnp.logical_not(late_u)
            pieces.append(jnp.where(keep_v & keep_u, data, 0.0).astype(BF))
            picks.append(
                jnp.where(target == first + (16 * down + right), 1.0, 0.0)
            )
    pick = jnp.concatenate(picks, axis=0)
    piece = jnp.concatenate(pieces, axis=0)
    pick = jnp.transpose(pick).astype(BF)
    out_ref[...] = jnp.dot(pick, piece, preferred_element_type=F32).astype(BF)


def total_kernel(recv_ref, out_ref):
    total = recv_ref[0:16, :].astype(F32)
    for source in range(1, 8):
        total = total + recv_ref[source * 16 : source * 16 + 16, :].astype(F32)
    for tile in range(2):
        for across in range(8):
            for k in range(4):
                row = tile * 8 + across
                out_ref[tile, k : k + 1, across * 256 : across * 256 + 256] = total[
                    row : row + 1, k * 256 : k * 256 + 256
                ]


PACK_BYTES = None
PACK_SCRATCH = [
    pltpu.VMEM((1, ROWS), I32),
    pltpu.VMEM((ROWS, DATA), BF),
    pltpu.VMEM((5, CHR, ROWS), I32),
    pltpu.VMEM((N_VIS, CAP, WIRE), BF),
    pltpu.SemaphoreType.DMA((10,)),
]
GRID_SCRATCH = [
    pltpu.VMEM((WIRE // 128, N_VIS * CAP + 8, 128), F32),
    pltpu.VMEM((5, BLK * CHR, N_VIS * CAP), F32),
    pltpu.VMEM((BLK, DATA, N_VIS * CAP), F32),
    pltpu.VMEM((BLK, 6, CHR, N_VIS * CAP), I32),
    pltpu.VMEM((BLK, 128, 128), F32),
    pltpu.VMEM((BLK, 2, SUB + 8, 128), F32),
    pltpu.VMEM((WIDE // 128, PIECES + 16, 128), F32),
]


def call(
    kernel, shape, dtype, spaces, scratch=(), flops=0, moved=0, out=pltpu.VMEM, limit=VMEM_BYTES
):
    specs = [pl.BlockSpec(memory_space=space) for space in spaces]
    return pl.pallas_call(
        kernel,
        out_shape=jax.ShapeDtypeStruct(shape, dtype),
        in_specs=specs,
        out_specs=pl.BlockSpec(memory_space=out),
        scratch_shapes=list(scratch),
        compiler_params=pltpu.CompilerParams(vmem_limit_bytes=limit),
        cost_estimate=pl.CostEstimate(flops=flops, bytes_accessed=moved, transcendentals=0),
    )


def on_device(
    vis_data,
    u_cell,
    v_cell,
    u_frac,
    v_frac,
    w_plane,
    block_route,
    kernel_taps,
    taper_gain,
    sub_tile,
    sub_anchor,
):
    vm, sm, hbm = pltpu.VMEM, pltpu.SMEM, pltpu.HBM
    packed = call(
        pack_kernel,
        (N_VIS, CAP, WIRE),
        BF,
        [hbm] * 7,
        scratch=PACK_SCRATCH,
        flops=1 << 30,
        moved=2 << 20,
        out=hbm,
        limit=PACK_BYTES,
    )(block_route.reshape(1, ROWS), vis_data, u_cell, v_cell, u_frac, v_frac, w_plane)
    rows = lax.all_to_all(
        packed, VIS, split_axis=0, concat_axis=0, tiled=True
    ).reshape(N_VIS * CAP, WIRE)

    taps = jnp.zeros((8, 128), F32).at[:TAPS].set(kernel_taps.T.astype(BF).astype(F32))
    taper = jnp.repeat(taper_gain, POLC, axis=1)
    pieces = call(
        grid_kernel,
        (PIECES // CAP, CAP, WIDE),
        BF,
        [sm, sm, vm, vm, vm],
        scratch=GRID_SCRATCH,
        flops=1 << 32,
        moved=2 << 20,
    )(sub_tile, sub_anchor, rows, taps, taper)
    pieces = lax.all_to_all(
        pieces,
        ("zl", "core", "tile"),
        split_axis=0,
        concat_axis=0,
        tiled=True,
    ).reshape(PIECES, WIDE)
    canvas = call(place_kernel, (PIECES, FLAT), BF, [vm], flops=1 << 27, moved=1 << 19)(pieces)
    canvas = lax.all_to_all(
        canvas.reshape(8, 16, FLAT), ("x", "zh"), split_axis=0, concat_axis=0, tiled=True
    ).reshape(PIECES, FLAT)
    return call(total_kernel, (2, 4, 2048), F32, [vm], moved=1 << 19)(canvas)


def solution(mesh):
    split = Mesh(
        mesh.devices.reshape(4, 2, 4, 2, 4), ("x", "zh", "zl", "core", "tile")
    )
    every = VIS + ("tile",)
    placed = (
        (P(every, None),)
        + (P(None, every),) * 5
        + (P(every, None), P(), P(), P(every, None), P(every, None))
    )
    return jax.shard_map(
        on_device, mesh=split, in_specs=placed, out_specs=P("tile", VIS, None), check_vma=False
    )
```
